256 devices in a mesh: inst: 32 (over y, z_hi, core), tp: 8 (over x, z_lo).
Axes of the slice: x: 4, y: 4, z: 8 (z_hi: 4, z_lo: 2; z = z_hi * 2 + z_lo), core: 2. Of those that a mesh axis runs over, the one named last changes fastest.
Arguments:
- queries: bfloat16 [3, 512, 8192], P(None, 'inst', 'tp'), may hold values from -18 to 18
- key_values: bfloat16 [512, 1024, 2048], P('inst', None, 'tp'), may hold values from -4 to 4
- new_key_values: bfloat16 [3, 512, 2048], P(None, 'inst', 'tp'), may hold values from -5 to 5
- cache_lengths: int32 [512], P('inst'), may hold values from 256 to 1021, as said below
- output_weight: bfloat16 [8192, 4096], P('tp'), may hold values from -0.0625 to 0.0625
- moving_requests: int32 [32, 4], P('inst'), may hold values from 0 to 15, as said below
- migration_plan: int32 [32, 4], replicated, may hold values from 0 to 31, as said below
- row_counts: int32 [3, 32, 4], replicated, may hold values from 1 to 32, as said below
- copied_rows: int32 [32, 4], P('inst'), may hold values from 0 to 160, as said below
- landing: bfloat16 [32, 4, 256, 2048], P('inst', None, None, 'tp'), may hold values from -6 to 6
Outputs:
- attended: bfloat16 [3, 512, 4096], P(None, 'inst', 'tp')
- landed: bfloat16 [32, 4, 256, 2048], P('inst', None, None, 'tp')
The draws below stay inside these ranges and needn't reach their ends.
Inputs may be any that keep to these rules, and one draw needn't show every extreme that they name: `cache_lengths`: one resident request has exactly 1021 valid rows. `moving_requests`: an instance's 4 entries are distinct. For every lane m, migration_plan[., m] is a permutation of the instances; an instance's destinations are distinct and never the instance itself. `row_counts`: some count equals 32. `copied_rows`: some slot holds exactly 160 rows.
All inputs are finite; a program needn't handle non-finite values.
Results may differ from the reference program's by a relative error of at most 0.0057.
Values may be sent and summed in bfloat16 or wider, within the bound.
A program may use at most 128 MiB of HBM per device.

```python
import math
import jax
import jax.numpy as jnp
from jax import lax

Q_HEADS = 64
KV_HEADS = 8
HEAD_DIM = 128
OUT_WIDTH = 4096
REQ_DEV = 16
CACHE = 1024
STEPS = 3
MOVING = 4
MOST_ROWS = 32
LAND_ROWS = 256
INSTS = 32
REQS = 512


def raw_queries(key):
    values = jax.random.normal(jax.random.fold_in(key, 72), (STEPS, REQS, KV_HEADS, Q_HEADS // KV_HEADS, HEAD_DIM), jnp.float32)
    return jnp.clip(values, -4.0, 4.0)


def draw_queries(key, part):
    values = raw_queries(key)
    return values.reshape(STEPS, REQS, Q_HEADS * HEAD_DIM).astype(jnp.bfloat16)


def draw_key_values(key, part):
    key = jax.random.fold_in(key, 3)
    shape = (REQS, CACHE, KV_HEADS, 2, HEAD_DIM)
    values = jnp.clip(jax.random.normal(key, shape, jnp.float32), -4.0, 4.0)
    return values.reshape(REQS, CACHE, KV_HEADS * 2 * HEAD_DIM).astype(jnp.bfloat16)


def draw_new_key_values(key, part):
    shared = raw_queries(key)[:, :, :, 1, :]
    key = jax.random.fold_in(key, 4)
    noise = jnp.clip(jax.random.normal(jax.random.fold_in(key, 1), shared.shape, jnp.float32), -4.0, 4.0)
    new_keys = 0.5 * shared + 0.7 * noise
    new_values = jnp.clip(jax.random.normal(jax.random.fold_in(key, 2), shared.shape, jnp.float32), -4.0, 4.0)
    stacked = jnp.stack([new_keys, new_values], axis=3)
    return stacked.reshape(STEPS, REQS, KV_HEADS * 2 * HEAD_DIM).astype(jnp.bfloat16)


def draw_cache_lengths(key, part):
    key = jax.random.fold_in(key, 6)
    lengths = jax.random.randint(jax.random.fold_in(key, 1), (REQS,), CACHE // 4, CACHE - STEPS + 1)
    longest = jax.random.randint(jax.random.fold_in(key, 2), (), 0, REQS)
    return jnp.where(jnp.arange(REQS) == longest, CACHE - STEPS, lengths).astype(jnp.int32)


def draw_moving_requests(key, part):
    key = jax.random.fold_in(key, 7)
    scores = jax.random.randint(key, (INSTS, REQ_DEV), 0, 1 << 20) * REQ_DEV + jnp.arange(REQ_DEV)[None, :]
    ordering = jnp.argsort(scores, axis=1)
    return ordering[:, :MOVING].astype(jnp.int32)


def draw_migration_plan(key, part):
    key = jax.random.fold_in(key, 8)
    ordering = jax.random.permutation(key, INSTS)
    placing = jnp.argsort(ordering)
    return ordering[(placing[:, None] + 1 + jnp.arange(MOVING)[None, :]) % INSTS].astype(jnp.int32)


def draw_row_counts(key, part):
    key = jax.random.fold_in(key, 9)
    upper = MOST_ROWS // 4
    base = jax.random.randint(jax.random.fold_in(key, 1), (STEPS, INSTS, MOVING), 1, upper + 1)
    heavy = jax.random.randint(jax.random.fold_in(key, 2), (INSTS, MOVING), 0, 3)
    counts = base * jnp.left_shift(jnp.ones_like(heavy), heavy)[None]
    chosen = jax.random.randint(jax.random.fold_in(key, 3), (), 0, INSTS)
    marker = (jnp.arange(STEPS)[:, None, None] == 0) & (jnp.arange(INSTS)[None, :, None] == chosen) & (jnp.arange(MOVING)[None, None, :] == 0)
    return jnp.where(marker, MOST_ROWS, counts).astype(jnp.int32)


def draw_copied_rows(key, part):
    key = jax.random.fold_in(key, 10)
    largest = LAND_ROWS - STEPS * MOST_ROWS
    rows = jax.random.randint(jax.random.fold_in(key, 1), (INSTS, MOVING), 0, largest + 1)
    chosen = jax.random.randint(jax.random.fold_in(key, 2), (), 0, INSTS * MOVING)
    return jnp.where(jnp.arange(INSTS * MOVING).reshape(INSTS, MOVING) == chosen, largest, rows).astype(jnp.int32)


def steps_of(stream_key, dims, split, low, high):
    level = 1.0
    for dim, parts in split:
        draws = jax.random.uniform(jax.random.fold_in(jax.random.fold_in(stream_key, 6), dim), (parts,), jnp.float32, low / len(split), high / len(split))
        level = level * jnp.repeat(jnp.exp(draws), dims[dim] // parts).reshape((-1,) + (1,) * (len(dims) - 1 - dim))
    return level


def scatter_about(stream_key, dims, width, bound, split=(), held_as=jnp.bfloat16):
    values = jax.random.normal(stream_key, dims, jnp.float32) * width
    if len(split) > 0:
        values = steps_of(stream_key, dims, split, -0.22, 0.18) * values
    return jnp.clip(values, min=-bound, max=bound).astype(held_as)


def setup_inputs(seed: int = 0) -> dict:
    key_of = jax.random.split(jax.random.key(seed), 11)
    return {
        "queries": draw_queries(jax.random.fold_in(key_of[10], 71), 0),
        "key_values": draw_key_values(jax.random.fold_in(key_of[10], 71), 0),
        "new_key_values": draw_new_key_values(jax.random.fold_in(key_of[10], 71), 0),
        "cache_lengths": draw_cache_lengths(jax.random.fold_in(key_of[10], 71), 0),
        "output_weight": scatter_about(key_of[4], (Q_HEADS * HEAD_DIM, OUT_WIDTH), (Q_HEADS * HEAD_DIM) ** -0.5, 0.0625, ((0, 8),)),
        "moving_requests": draw_moving_requests(jax.random.fold_in(key_of[10], 71), 0),
        "migration_plan": draw_migration_plan(jax.random.fold_in(key_of[10], 71), 0),
        "row_counts": draw_row_counts(jax.random.fold_in(key_of[10], 71), 0),
        "copied_rows": draw_copied_rows(jax.random.fold_in(key_of[10], 71), 0),
        "landing": scatter_about(key_of[9], (INSTS, MOVING, LAND_ROWS, KV_HEADS * 2 * HEAD_DIM), 1.0, 6.0, ((0, 32), (3, 8))),
    }


def request_context(packed):
    query, stored, newest, length = packed
    group_size = Q_HEADS // KV_HEADS
    factor = 1.0 / math.sqrt(HEAD_DIM)
    query_heads = query.astype(jnp.float32).reshape(STEPS, KV_HEADS, group_size, HEAD_DIM)
    stored = stored.astype(jnp.float32).reshape(CACHE, KV_HEADS, 2, HEAD_DIM)
    newest = newest.astype(jnp.float32).reshape(STEPS, KV_HEADS, 2, HEAD_DIM)
    old_scores = jnp.einsum('skgd,lkd->skgl', query_heads, stored[:, :, 0], precision=lax.Precision.HIGHEST) * factor
    new_scores = jnp.einsum('skgd,tkd->skgt', query_heads, newest[:, :, 0], precision=lax.Precision.HIGHEST) * factor
    old_mask = (jnp.arange(CACHE, dtype=jnp.int32) < length)[None, None, None, :]
    step_ids = jnp.arange(STEPS, dtype=jnp.int32)
    new_mask = (step_ids[None, :] <= step_ids[:, None])[:, None, None, :]
    highest = jnp.maximum(lax.optimization_barrier(jnp.max(jnp.where(old_mask, old_scores, -jnp.inf), axis=-1)), lax.optimization_barrier(jnp.max(jnp.where(new_mask, new_scores, -jnp.inf), axis=-1)))
    old_exp = jnp.where(old_mask, jnp.exp(old_scores - highest[..., None]), 0.0)
    new_exp = jnp.where(new_mask, jnp.exp(new_scores - highest[..., None]), 0.0)
    denominator = lax.optimization_barrier(jnp.sum(old_exp, axis=-1)) + lax.optimization_barrier(jnp.sum(new_exp, axis=-1))
    old_weight = lax.optimization_barrier((old_exp / denominator[..., None]).astype(jnp.bfloat16)).astype(jnp.float32)
    new_weight = lax.optimization_barrier((new_exp / denominator[..., None]).astype(jnp.bfloat16)).astype(jnp.float32)
    context = jnp.einsum('skgl,lkd->skgd', old_weight, stored[:, :, 1], precision=lax.Precision.HIGHEST)
    context = context + jnp.einsum('skgt,tkd->skgd', new_weight, newest[:, :, 1], precision=lax.Precision.HIGHEST)
    return context.reshape(STEPS, Q_HEADS * HEAD_DIM).astype(jnp.bfloat16)

def reference(queries, key_values, new_key_values, cache_lengths, output_weight, moving_requests, migration_plan, row_counts, copied_rows, landing):
    contexts = lax.map(request_context, (jnp.swapaxes(queries, 0, 1), key_values, jnp.swapaxes(new_key_values, 0, 1), cache_lengths))
    context = jnp.swapaxes(contexts, 0, 1)
    attended = jnp.dot(context.reshape(STEPS * REQS, Q_HEADS * HEAD_DIM), output_weight, preferred_element_type=jnp.float32)
    attended = attended.reshape(STEPS, REQS, OUT_WIDTH).astype(jnp.bfloat16)
    instances = migration_plan.shape[0]
    inst_ids = jnp.arange(instances, dtype=jnp.int32)
    lanes = jnp.arange(MOVING, dtype=jnp.int32)
    matches = migration_plan[:, None, :] == inst_ids[None, :, None]
    senders = lax.optimization_barrier(jnp.sum(jnp.where(matches, inst_ids[:, None, None], 0), axis=0)).astype(jnp.int32)
    overall = lax.optimization_barrier(jnp.sum(row_counts, axis=0)).astype(jnp.int32)
    offsets = (jnp.cumsum(row_counts, axis=0) - row_counts).astype(jnp.int32)
    requests = (senders * REQ_DEV + moving_requests[senders, lanes[None, :]]).astype(jnp.int32)
    counts_in = row_counts[:, senders, lanes[None, :]]
    offsets_in = offsets[:, senders, lanes[None, :]]
    totals_in = overall[senders, lanes[None, :]]
    span = jnp.arange(MOST_ROWS, dtype=jnp.int32)
    starts = cache_lengths[requests][None] - totals_in[None] + offsets_in
    source_rows = jnp.clip(starts[..., None] + span, 0, CACHE - 1).astype(jnp.int32)
    moved = key_values[requests[None, :, :, None], source_rows]
    target_rows = copied_rows[None, :, :, None] + offsets_in[..., None] + span
    target_rows = jnp.where(span < counts_in[..., None], target_rows, LAND_ROWS).astype(jnp.int32)
    dest_ids = inst_ids[None, :, None, None]
    lane_ids = lanes[None, None, :, None]
    landed = landing.at[dest_ids, lane_ids, target_rows].set(moved, mode='drop')
    return (attended, landed)
```

```python
import functools
import math

import jax
import jax.numpy as jnp
from jax import lax
from jax.experimental import pallas as pl
from jax.experimental.pallas import tpu as pltpu
from jax.sharding import PartitionSpec as P

HEAD_DIM = 128
STEPS = 3
HEADS = 8
REQS = 16
CACHE = 1024
MOVING = 4
MOST_ROWS = 32
LANE_ROWS = STEPS * MOST_ROWS
LAND_ROWS = 256
INSTS = 32
CHIPS = 16
TP = 8
OUT_WIDTH = 4096
ROWS = STEPS * HEADS
TOKENS = STEPS * REQS
WIDE = OUT_WIDTH // 4
NARROW = OUT_WIDTH // TP
GROUP = 4
GROUPS = REQS // GROUP
TILE = 16
TILES = CACHE // TILE
WINDOW = LANE_ROWS + TILE
LOW = -1e30
SCALE = math.log2(math.e) / math.sqrt(HEAD_DIM)
F32 = jnp.float32
BF16 = jnp.bfloat16
I32 = jnp.int32


def iota(shape, dim):
    return lax.broadcasted_iota(I32, shape, dim)


def wait_bytes(ref, sem):
    pltpu.make_async_copy(ref, ref, sem).wait()


def main_kernel(
    lengths_hbm,
    moving_hbm,
    copied_hbm,
    queries_hbm,
    newest_hbm,
    cache_hbm,
    weight_hbm,
    plan_hbm,
    counts_hbm,
    landing_hbm,
    attended,
    landed,
    lengths,
    moving,
    copied,
    queries,
    newest,
    cache,
    weight,
    plan,
    counts,
    landing,
    meta_vec,
    meta,
    ordered,
    regroup,
    new_scores,
    acc,
    top,
    norm,
    scatter_out,
    scatter_in,
    forward_out,
    forward_in,
    wide_out,
    wide_in,
    wide_own,
    narrow_out,
    narrow_in,
    small_sem,
    cache_sem,
    weight_sem,
    landing_sem,
    meta_sem,
    scatter_sem,
    forward_sem,
    wide_send_sem,
    wide_recv_sem,
    narrow_sem,
):
    me = lax.axis_index("inst")
    tp = lax.axis_index("tp")
    chip = me // 2
    core = lax.rem(me, 2)
    column = tp // 2
    side = lax.rem(tp, 2)
    lane = chip // 4

    barrier = pltpu.get_barrier_semaphore()

    def greet(o, carry):
        pl.semaphore_signal(
            barrier, inc=1, device_id={"inst": lax.rem(me + o, INSTS)}
        )
        return carry

    small = [
        pltpu.make_async_copy(src, dst, small_sem.at[n])
        for n, (src, dst) in enumerate(
            [
                (queries_hbm, queries),
                (newest_hbm, newest),
                (plan_hbm, plan),
                (counts_hbm, counts),
                (lengths_hbm, lengths),
                (moving_hbm, moving),
                (copied_hbm, copied),
            ]
        )
    ]
    for copy in small:
        copy.start()
    cache_loads = []
    for g in range(GROUPS):
        part = pl.ds(g * GROUP * TILES, GROUP * TILES)
        cache_loads.append(
            pltpu.make_async_copy(cache_hbm.at[part], cache.at[part], cache_sem.at[g])
        )
        cache_loads[-1].start()
    lax.fori_loop(1, INSTS, greet, 0)
    for k in range(3):
        other = lax.rem(column + 1 + k, 4)
        pl.semaphore_signal(barrier, inc=1, device_id={"tp": other * 2 + side})
    pl.semaphore_signal(barrier, inc=1, device_id={"tp": column * 2 + 1 - side})
    weight_loads = []
    for k in range(4):
        target = lax.rem(column + 1 + k, 4)
        weight_loads.append(
            pltpu.make_async_copy(
                weight_hbm.at[:, pl.ds(pl.multiple_of(target * WIDE, WIDE), WIDE)],
                weight.at[k],
                weight_sem.at[k],
            )
        )
        weight_loads[-1].start()
    landing_load = pltpu.make_async_copy(landing_hbm, landing, landing_sem.at[0])
    landing_load.start()

    for copy in small:
        copy.wait()
    inst_rows = iota((INSTS, INSTS), 0)
    inst_cols = iota((INSTS, INSTS), 1)
    total = counts[0] + counts[1] + counts[2]
    for m in range(MOVING):
        hit = plan[m : m + 1, :] == inst_rows
        sender = jnp.sum(jnp.where(hit, inst_cols, 0), axis=1, keepdims=True)
        meta_vec[0:INSTS, m : m + 1] = jnp.minimum(sender, INSTS - 1)
        meta_vec[0:INSTS, MOVING + m : MOVING + m + 1] = jnp.sum(
            jnp.where(hit, total[m : m + 1, :], 0), axis=1, keepdims=True
        )
    meta_vec[INSTS : INSTS + MOVING, 0:INSTS] = total
    meta_load = pltpu.make_async_copy(meta_vec, meta, meta_sem.at[0])
    meta_load.start()

    stacked = jnp.concatenate(
        [
            queries[s, :, h * HEAD_DIM : (h + 1) * HEAD_DIM]
            for s in range(STEPS)
            for h in range(HEADS)
        ],
        axis=0,
    )
    pick = iota((ROWS, REQS * ROWS), 1) - REQS * iota((ROWS, REQS * ROWS), 0)
    order = jnp.concatenate(
        [(pick == b).astype(F32) for b in range(REQS)], axis=0
    ).astype(BF16)
    ordered[...] = jnp.dot(order, stacked, preferred_element_type=F32)
    back = iota((REQS, REQS * ROWS), 1) - ROWS * iota((REQS, REQS * ROWS), 0)
    for h in range(HEADS):
        for s in range(STEPS):
            n = (h * STEPS + s) * REQS
            regroup[n : n + REQS, :] = (back == s * HEADS + h).astype(F32).astype(BF16)
    fresh = lax.dot_general(
        ordered[...].astype(BF16),
        newest[:, :HEAD_DIM],
        (((1,), (1,)), ((), ())),
        preferred_element_type=F32,
    )
    position = iota((ROWS, TOKENS), 1)
    causal = (position >> 4) <= (iota((ROWS, TOKENS), 0) >> 3)
    for b in range(REQS):
        rows = slice(b * ROWS, (b + 1) * ROWS)
        valid = causal & ((position & (REQS - 1)) == b)
        new_scores[rows, :] = jnp.where(valid, fresh[rows] * SCALE, LOW)

    def attend_group(g):
        members = range(g * GROUP, (g + 1) * GROUP)
        rows = [slice(b * ROWS, (b + 1) * ROWS) for b in members]
        stored = [
            cache[b * TILES : (b + 1) * TILES].reshape(CACHE, 2 * HEAD_DIM) for b in members
        ]
        scores = [
            lax.dot_general(
                ordered[r, :].astype(BF16),
                kv[:, :HEAD_DIM],
                (((1,), (1,)), ((), ())),
                preferred_element_type=F32,
            )
            for r, kv in zip(rows, stored)
        ]
        scores = [
            jnp.where(iota((ROWS, CACHE), 1) < lengths[b], x * SCALE, LOW)
            for b, x in zip(members, scores)
        ]
        highest = [
            jnp.maximum(
                jnp.max(x, axis=1, keepdims=True),
                jnp.max(new_scores[r, :], axis=1, keepdims=True),
            )
            for r, x in zip(rows, scores)
        ]
        weights = [jnp.exp2(x - h) for x, h in zip(scores, highest)]
        sums = [jnp.sum(w, axis=1, keepdims=True) for w in weights]
        outs = [
            jnp.dot(w.astype(BF16), kv[:, HEAD_DIM:], preferred_element_type=F32)
            for w, kv in zip(weights, stored)
        ]
        for r, h, n, o in zip(rows, highest, sums, outs):
            top[r, :] = jnp.broadcast_to(h, (ROWS, HEAD_DIM))
            norm[r, :] = jnp.broadcast_to(n, (ROWS, HEAD_DIM))
            acc[r, :] = o

    for g in range(GROUPS - 1):
        cache_loads[g].wait()
        attend_group(g)
    cache_loads[GROUPS - 1].wait()

    meta_load.wait()
    tail_rows = iota((LANE_ROWS, WINDOW), 0)
    tail_cols = iota((LANE_ROWS, WINDOW), 1)
    for m in range(MOVING):
        request = moving[0, m]
        total = meta[INSTS + m, me]
        start = lengths[request] - total
        first = jnp.minimum(start // TILE, TILES - WINDOW // TILE)
        window = jnp.concatenate(
            [cache[request * TILES + first + t] for t in range(WINDOW // TILE)], axis=0
        )
        shift = (tail_cols - tail_rows == start - first * TILE) & (tail_rows < total)
        tail = jnp.dot(
            shift.astype(F32).astype(BF16), window, preferred_element_type=F32
        ).astype(BF16)
        for q in range(12):
            r, c = (q // 2) * 16, (q % 2) * 128
            scatter_out[m * 12 + q] = tail[r : r + 16, c : c + 128]

    pl.semaphore_wait(barrier, INSTS - 1 + 3 + 1)

    def scatter_two(target_chip, sem):
        return pltpu.make_async_remote_copy(
            src_ref=scatter_out.at[pl.ds(target_chip * 3, 2)],
            dst_ref=scatter_in.at[me],
            send_sem=sem,
            recv_sem=scatter_sem.at[0],
            device_id={"inst": target_chip * 2},
        )

    def scatter_one(target_chip, sem):
        return pltpu.make_async_remote_copy(
            src_ref=scatter_out.at[pl.ds(target_chip * 3 + 2, 1)],
            dst_ref=scatter_in.at[me, pl.ds(0, 1)],
            send_sem=sem,
            recv_sem=scatter_sem.at[0],
            device_id={"inst": target_chip * 2 + 1},
        )

    def scatter(o, carry):
        target_chip = lax.rem(chip + o, CHIPS)
        scatter_two(target_chip, scatter_sem.at[1]).start()
        scatter_one(target_chip, scatter_sem.at[1]).start()
        return carry

    lax.fori_loop(1, CHIPS, scatter, 0)

    @pl.when(core == 0)
    def _():
        scatter_one(chip, scatter_sem.at[2]).start()
        scatter_in[me] = scatter_out[pl.ds(chip * 3, 2)]

    @pl.when(core == 1)
    def _():
        scatter_two(chip, scatter_sem.at[2]).start()
        scatter_in[me, 0] = scatter_out[chip * 3 + 2]

    attend_group(GROUPS - 1)

    late = jnp.exp2(new_scores[...] - top[:, :TOKENS])
    whole = norm[...] + jnp.sum(late, axis=1, keepdims=True)
    context = acc[...] + jnp.dot(
        late.astype(BF16), newest[:, HEAD_DIM:], preferred_element_type=F32
    )
    context = (context / whole).astype(BF16)
    context = jnp.dot(regroup[...], context, preferred_element_type=F32).astype(BF16)
    context = jnp.concatenate(
        [context[h * TOKENS : (h + 1) * TOKENS] for h in range(HEADS)], axis=1
    )

    wide_sends = []

    def project(k):
        weight_loads[k].wait()
        partial = jnp.dot(context, weight[k], preferred_element_type=F32)
        if k < 3:
            wide_out[k] = partial.astype(BF16)
            copy = pltpu.make_async_remote_copy(
                src_ref=wide_out.at[k],
                dst_ref=wide_in.at[k],
                send_sem=wide_send_sem.at[k],
                recv_sem=wide_recv_sem.at[k],
                device_id={"tp": lax.rem(column + 1 + k, 4) * 2 + side},
            )
            copy.start()
            wide_sends.append(copy)
        else:
            wide_own[...] = partial

    for k in range(4):
        project(k)

    def forward_two(target):
        return pltpu.make_async_remote_copy(
            src_ref=forward_out.at[target],
            dst_ref=forward_in.at[pl.ds(chip * 3, 2)],
            send_sem=forward_sem.at[1],
            recv_sem=forward_sem.at[0],
            device_id={"inst": target},
        )

    def forward_one(target):
        return pltpu.make_async_remote_copy(
            src_ref=forward_out.at[target, pl.ds(0, 1)],
            dst_ref=forward_in.at[pl.ds(chip * 3 + 2, 1)],
            send_sem=forward_sem.at[1],
            recv_sem=forward_sem.at[0],
            device_id={"inst": target},
        )

    @pl.when(core == 0)
    def _():
        wait_bytes(scatter_in.at[pl.ds(0, INSTS - 1)], scatter_sem.at[0])

        for d in range(INSTS):
            forward_out[d] = scatter_in[meta[d, lane]]

        def forward(o, carry):
            forward_two(lax.rem(me + o, INSTS)).start()
            return carry

        lax.fori_loop(1, INSTS, forward, 0)
        forward_in[pl.ds(chip * 3, 2)] = scatter_in[meta[me, lane]]

    @pl.when(core == 1)
    def _():
        wait_bytes(scatter_in.at[pl.ds(0, INSTS - 1), 0], scatter_sem.at[0])

        for d in range(INSTS):
            forward_out[d, 0] = scatter_in[meta[d, lane], 0]

        def forward(o, carry):
            forward_one(lax.rem(me + o, INSTS)).start()
            return carry

        lax.fori_loop(1, INSTS, forward, 0)
        forward_in[chip * 3 + 2] = scatter_in[meta[me, lane], 0]

    for k in range(3):
        pltpu.make_async_copy(wide_in.at[k], wide_in.at[k], wide_recv_sem.at[k]).wait()
    total = wide_own[...]
    for k in range(3):
        total = total + wide_in[k].astype(F32)
    left, right = total[:, :NARROW], total[:, NARROW:]
    narrow_out[...] = jnp.where(side == 0, right, left).astype(BF16)
    narrow_send = pltpu.make_async_remote_copy(
        src_ref=narrow_out,
        dst_ref=narrow_in,
        send_sem=narrow_sem.at[0],
        recv_sem=narrow_sem.at[1],
        device_id={"tp": column * 2 + 1 - side},
    )
    narrow_send.start()
    own = jnp.where(side == 0, left, right)
    narrow_send.wait_recv()
    attended[...] = (own + narrow_in[...].astype(F32)).astype(BF16)

    landing_load.wait()

    @pl.when(core == 0)
    def _():
        wait_bytes(forward_in.at[pl.ds(0, 46)], forward_sem.at[0])

    @pl.when(core == 1)
    def _():
        wait_bytes(forward_in.at[pl.ds(0, 47)], forward_sem.at[0])

    land_rows = iota((LAND_ROWS, LANE_ROWS), 0)
    land_cols = iota((LAND_ROWS, LANE_ROWS), 1)
    target_rows = iota((LAND_ROWS, 2 * HEAD_DIM), 0)
    for m in range(MOVING):
        first = copied[0, m]
        total_in = meta[me, MOVING + m]
        arrived = jnp.concatenate(
            [
                jnp.concatenate(
                    [forward_in[m * 12 + 2 * r], forward_in[m * 12 + 2 * r + 1]], axis=1
                )
                for r in range(6)
            ],
            axis=0,
        )
        place = (land_rows - land_cols == first).astype(F32).astype(BF16)
        placed = jnp.dot(place, arrived, preferred_element_type=F32).astype(BF16)
        fits = (target_rows >= first) & (target_rows < first + total_in)
        landed[m] = jnp.where(fits, placed, landing[m])

    for copy in wide_sends:
        copy.wait_send()
    narrow_send.wait_send()
    wait_bytes(scatter_out.at[pl.ds(0, 45)], scatter_sem.at[1])

    @pl.when(core == 0)
    def _():
        wait_bytes(scatter_out.at[pl.ds(0, 1)], scatter_sem.at[2])
        wait_bytes(forward_out.at[pl.ds(0, INSTS - 1)], forward_sem.at[1])

    @pl.when(core == 1)
    def _():
        wait_bytes(scatter_out.at[pl.ds(0, 2)], scatter_sem.at[2])
        wait_bytes(forward_out.at[pl.ds(0, INSTS - 1), 0], forward_sem.at[1])


def on_device(
    queries,
    key_values,
    new_key_values,
    cache_lengths,
    output_weight,
    moving_requests,
    migration_plan,
    row_counts,
    copied_rows,
    landing,
):
    in_hbm = pl.BlockSpec(memory_space=pltpu.HBM)
    dma = pltpu.SemaphoreType.DMA
    attended, landed = pl.pallas_call(
        main_kernel,
        out_shape=(
            jax.ShapeDtypeStruct((TOKENS, NARROW), BF16),
            jax.ShapeDtypeStruct((MOVING, LAND_ROWS, 2 * HEAD_DIM), BF16),
        ),
        in_specs=[in_hbm] * 10,
        out_specs=(
            pl.BlockSpec(memory_space=pltpu.VMEM),
            pl.BlockSpec(memory_space=pltpu.VMEM),
        ),
        scratch_shapes=[
            pltpu.SMEM((REQS,), I32),
            pltpu.SMEM((1, MOVING), I32),
            pltpu.SMEM((1, MOVING), I32),
            pltpu.VMEM((STEPS, REQS, HEADS * HEAD_DIM), BF16),
            pltpu.VMEM((TOKENS, 2 * HEAD_DIM), BF16),
            pltpu.VMEM((REQS * TILES, TILE, 2 * HEAD_DIM), BF16),
            pltpu.VMEM((4, HEADS * HEAD_DIM, WIDE), BF16),
            pltpu.VMEM((MOVING, INSTS), I32),
            pltpu.VMEM((STEPS, MOVING, INSTS), I32),
            pltpu.VMEM((MOVING, LAND_ROWS, 2 * HEAD_DIM), BF16),
            pltpu.VMEM((40, 128), I32),
            pltpu.SMEM((40, 128), I32),
            pltpu.VMEM((REQS * ROWS, HEAD_DIM), F32),
            pltpu.VMEM((REQS * ROWS, REQS * ROWS), BF16),
            pltpu.VMEM((REQS * ROWS, TOKENS), F32),
            pltpu.VMEM((REQS * ROWS, HEAD_DIM), F32),
            pltpu.VMEM((REQS * ROWS, HEAD_DIM), F32),
            pltpu.VMEM((REQS * ROWS, HEAD_DIM), F32),
            pltpu.VMEM((48, 16, 128), BF16),
            pltpu.VMEM((INSTS, 2, 16, 128), BF16),
            pltpu.VMEM((INSTS, 2, 16, 128), BF16),
            pltpu.VMEM((48, 16, 128), BF16),
            pltpu.VMEM((3, TOKENS, WIDE), BF16),
            pltpu.VMEM((3, TOKENS, WIDE), BF16),
            pltpu.VMEM((TOKENS, WIDE), F32),
            pltpu.VMEM((TOKENS, NARROW), BF16),
            pltpu.VMEM((TOKENS, NARROW), BF16),
            dma((7,)),
            dma((GROUPS,)),
            dma((4,)),
            dma((1,)),
            dma((1,)),
            dma((3,)),
            dma((2,)),
            dma((3,)),
            dma((3,)),
            dma((2,)),
        ],
        compiler_params=pltpu.CompilerParams(
            collective_id=0,
            has_side_effects=True,
            vmem_limit_bytes=40 * 1024 * 1024,
        ),
    )(
        *(
            pltpu.with_memory_space_constraint(x, pltpu.HBM)
            for x in (
                cache_lengths,
                moving_requests,
                copied_rows,
                queries,
                new_key_values.reshape(TOKENS, 2 * HEAD_DIM),
                key_values.reshape(REQS * TILES, TILE, 2 * HEAD_DIM),
                output_weight,
                migration_plan.T,
                row_counts.transpose(0, 2, 1),
                landing[0],
            )
        )
    )
    return attended.reshape(STEPS, REQS, NARROW), landed[None]


def solution(mesh):
    placed = (
        P(None, "inst", "tp"),
        P("inst", None, "tp"),
        P(None, "inst", "tp"),
        P("inst"),
        P("tp", None),
        P("inst", None),
        P(),
        P(),
        P("inst", None),
        P("inst", None, None, "tp"),
    )
    return jax.shard_map(
        on_device,
        mesh=mesh,
        in_specs=placed,
        out_specs=(P(None, "inst", "tp"), P("inst", None, None, "tp")),
        check_vma=False,
    )
```

```python
import functools
import math

import jax
import jax.numpy as jnp
from jax import lax
from jax.experimental import pallas as pl
from jax.experimental.pallas import tpu as pltpu
from jax.sharding import PartitionSpec as P

HEAD_DIM = 128
STEPS = 3
HEADS = 8
REQS = 16
CACHE = 1024
MOVING = 4
MOST_ROWS = 32
LANE_ROWS = STEPS * MOST_ROWS
LAND_ROWS = 256
INSTS = 32
PLANE = 8
HALF = LANE_ROWS // 2
TP = 8
OUT_WIDTH = 4096
ROWS = STEPS * HEADS
TOKENS = STEPS * REQS
WIDE = OUT_WIDTH // 4
NARROW = OUT_WIDTH // TP
GROUP = 4
GROUPS = REQS // GROUP
TILE = 16
TILES = CACHE // TILE
WINDOW = LANE_ROWS + TILE
LOW = -1e30
SCALE = math.log2(math.e) / math.sqrt(HEAD_DIM)
F32 = jnp.float32
BF16 = jnp.bfloat16
I32 = jnp.int32


def iota(shape, dim):
    return lax.broadcasted_iota(I32, shape, dim)


def wait_bytes(ref, sem):
    pltpu.make_async_copy(ref, ref, sem).wait()


def main_kernel(
    lengths_hbm,
    moving_hbm,
    copied_hbm,
    queries_hbm,
    newest_hbm,
    cache_hbm,
    weight_hbm,
    plan_hbm,
    counts_hbm,
    landing_hbm,
    attended,
    landed,
    lengths,
    moving,
    copied,
    queries,
    newest,
    cache,
    weight,
    plan,
    counts,
    landing,
    meta_vec,
    meta,
    ordered,
    regroup,
    new_scores,
    acc,
    top,
    norm,
    tails,
    held,
    inside,
    upward,
    downward,
    arrived,
    wide_out,
    wide_in,
    wide_own,
    narrow_out,
    narrow_in,
    small_sem,
    cache_sem,
    weight_sem,
    landing_sem,
    meta_sem,
    scatter_sem,
    forward_sem,
    wide_send_sem,
    wide_recv_sem,
    narrow_sem,
):
    me = lax.axis_index("inst")
    tp = lax.axis_index("tp")
    depth = lax.rem(me // 2, 4)
    spot = (me // 8) * 2 + lax.rem(me, 2)
    lane = me // 8
    column = tp // 2
    side = lax.rem(tp, 2)

    def device(place, plane):
        return ((place // 2) * 4 + plane) * 2 + lax.rem(place, 2)

    above, below = lax.rem(depth + 1, 4), lax.rem(depth + 3, 4)

    barrier = pltpu.get_barrier_semaphore()

    def greet(o, carry):
        place = lax.rem(spot + o, PLANE)
        for plane in (above, below):
            pl.semaphore_signal(
                barrier, inc=1, device_id={"inst": device(place, plane)}
            )
        return carry

    def greet_plane(o, carry):
        place = lax.rem(spot + o, PLANE)
        pl.semaphore_signal(barrier, inc=1, device_id={"inst": device(place, depth)})
        return carry

    lax.fori_loop(0, PLANE, greet, 0)
    lax.fori_loop(1, PLANE, greet_plane, 0)
    for k in range(3):
        other = lax.rem(column + 1 + k, 4)
        pl.semaphore_signal(barrier, inc=1, device_id={"tp": other * 2 + side})
    pl.semaphore_signal(barrier, inc=1, device_id={"tp": column * 2 + 1 - side})

    small = [
        pltpu.make_async_copy(src, dst, small_sem.at[n])
        for n, (src, dst) in enumerate(
            [
                (queries_hbm, queries),
                (newest_hbm, newest),
                (plan_hbm, plan),
                (counts_hbm, counts),
                (lengths_hbm, lengths),
                (moving_hbm, moving),
                (copied_hbm, copied),
            ]
        )
    ]
    for copy in small:
        copy.start()
    cache_loads = []
    for g in range(GROUPS):
        part = pl.ds(g * GROUP * TILES, GROUP * TILES)
        cache_loads.append(
            pltpu.make_async_copy(cache_hbm.at[part], cache.at[part], cache_sem.at[g])
        )
        cache_loads[-1].start()
    weight_loads = []
    for k in range(4):
        target = lax.rem(column + 1 + k, 4)
        weight_loads.append(
            pltpu.make_async_copy(
                weight_hbm.at[:, pl.ds(pl.multiple_of(target * WIDE, WIDE), WIDE)],
                weight.at[k],
                weight_sem.at[k],
            )
        )
    landing_load = pltpu.make_async_copy(landing_hbm, landing, landing_sem.at[0])

    for copy in small:
        copy.wait()
    inst_rows = iota((INSTS, INSTS), 0)
    inst_cols = iota((INSTS, INSTS), 1)
    total = counts[0] + counts[1] + counts[2]
    for m in range(MOVING):
        hit = plan[m : m + 1, :] == inst_rows
        sender = jnp.sum(jnp.where(hit, inst_cols, 0), axis=1, keepdims=True)
        sender = jnp.minimum(sender, INSTS - 1)
        place = ((sender >> 3) << 1) + (sender & 1)
        plane = (sender >> 1) & 3
        offset = (plane - depth) & 3
        away = (plane - ((inst_rows[:, :1] >> 1) & 3)) & 3
        low, high = 2 * place, 2 * place + 1
        from_below, from_above = 2 * PLANE + place, 3 * PLANE + place
        columns = (
            jnp.where(offset == 3, from_below, low),
            jnp.where(offset == 1, from_above, high),
            jnp.where(offset == 3, from_below, high),
            jnp.where(offset == 1, from_above, low),
            jnp.sum(jnp.where(hit, total[m : m + 1, :], 0), axis=1, keepdims=True),
            jnp.where(away == 1, 3, jnp.where(away == 2, 2, 0)),
            jnp.where(away == 3, 2, jnp.where(away == 2, 3, 1)),
        )
        for n, values in enumerate(columns):
            n = n * MOVING + m
            meta_vec[0:INSTS, n : n + 1] = values
    meta_vec[INSTS : INSTS + MOVING, 0:INSTS] = total
    meta_load = pltpu.make_async_copy(meta_vec, meta, meta_sem.at[0])
    meta_load.start()

    stacked = jnp.concatenate(
        [
            queries[s, :, h * HEAD_DIM : (h + 1) * HEAD_DIM]
            for s in range(STEPS)
            for h in range(HEADS)
        ],
        axis=0,
    )
    pick = iota((ROWS, REQS * ROWS), 1) - REQS * iota((ROWS, REQS * ROWS), 0)
    order = jnp.concatenate(
        [(pick == b).astype(F32) for b in range(REQS)], axis=0
    ).astype(BF16)
    ordered[...] = jnp.dot(order, stacked, preferred_element_type=F32)
    back = iota((REQS, REQS * ROWS), 1) - ROWS * iota((REQS, REQS * ROWS), 0)
    for h in range(HEADS):
        for s in range(STEPS):
            n = (h * STEPS + s) * REQS
            regroup[n : n + REQS, :] = (back == s * HEADS + h).astype(F32).astype(BF16)
    fresh = lax.dot_general(
        ordered[...].astype(BF16),
        newest[:, :HEAD_DIM],
        (((1,), (1,)), ((), ())),
        preferred_element_type=F32,
    )
    position = iota((ROWS, TOKENS), 1)
    causal = (position >> 4) <= (iota((ROWS, TOKENS), 0) >> 3)
    for b in range(REQS):
        rows = slice(b * ROWS, (b + 1) * ROWS)
        valid = causal & ((position & (REQS - 1)) == b)
        new_scores[rows, :] = jnp.where(valid, fresh[rows] * SCALE, LOW)

    def attend_group(g):
        members = range(g * GROUP, (g + 1) * GROUP)
        rows = [slice(b * ROWS, (b + 1) * ROWS) for b in members]
        stored = [
            cache[b * TILES : (b + 1) * TILES].reshape(CACHE, 2 * HEAD_DIM) for b in members
        ]
        scores = [
            lax.dot_general(
                ordered[r, :].astype(BF16),
                kv[:, :HEAD_DIM],
                (((1,), (1,)), ((), ())),
                preferred_element_type=F32,
            )
            for r, kv in zip(rows, stored)
        ]
        scores = [
            jnp.where(iota((ROWS, CACHE), 1) < lengths[b], x * SCALE, LOW)
            for b, x in zip(members, scores)
        ]
        highest = [
            jnp.maximum(
                jnp.max(x, axis=1, keepdims=True),
                jnp.max(new_scores[r, :], axis=1, keepdims=True),
            )
            for r, x in zip(rows, scores)
        ]
        weights = [jnp.exp2(x - h) for x, h in zip(scores, highest)]
        sums = [jnp.sum(w, axis=1, keepdims=True) for w in weights]
        outs = [
            jnp.dot(w.astype(BF16), kv[:, HEAD_DIM:], preferred_element_type=F32)
            for w, kv in zip(weights, stored)
        ]
        for r, h, n, o in zip(rows, highest, sums, outs):
            top[r, :] = jnp.broadcast_to(h, (ROWS, HEAD_DIM))
            norm[r, :] = jnp.broadcast_to(n, (ROWS, HEAD_DIM))
            acc[r, :] = o

    for g in range(GROUPS - 1):
        cache_loads[g].wait()
        if g == 1:
            for load in weight_loads:
                load.start()
            landing_load.start()
        attend_group(g)
    cache_loads[GROUPS - 1].wait()

    meta_load.wait()
    tail_rows = iota((LANE_ROWS, WINDOW), 0)
    tail_cols = iota((LANE_ROWS, WINDOW), 1)
    for m in range(MOVING):
        request = moving[0, m]
        total = meta[INSTS + m, me]
        start = lengths[request] - total
        first = jnp.minimum(start // TILE, TILES - WINDOW // TILE)
        window = jnp.concatenate(
            [cache[request * TILES + first + t] for t in range(WINDOW // TILE)], axis=0
        )
        shift = (tail_cols - tail_rows == start - first * TILE) & (tail_rows < total)
        tail = jnp.dot(
            shift.astype(F32).astype(BF16), window, preferred_element_type=F32
        ).astype(BF16)
        for c in range(2):
            for n in range(2):
                tails[2 * m + c, n] = tail[
                    n * HALF : (n + 1) * HALF, c * HEAD_DIM : (c + 1) * HEAD_DIM
                ]

    pl.semaphore_wait(barrier, 3 * PLANE - 1 + 3 + 1)

    def send(src, dst, place, plane, sems):
        pltpu.make_async_remote_copy(
            src_ref=src,
            dst_ref=dst,
            send_sem=sems.at[0],
            recv_sem=sems.at[1],
            device_id={"inst": device(place, plane)},
        ).start()

    def scatter(o, carry):
        place = lax.rem(spot + o, PLANE)
        send(tails.at[place, 0], held.at[2 * PLANE + spot], place, above, scatter_sem)
        send(tails.at[place, 1], held.at[3 * PLANE + spot], place, below, scatter_sem)
        return carry

    def scatter_plane(o, carry):
        place = lax.rem(spot + o, PLANE)
        send(tails.at[place], held.at[pl.ds(2 * spot, 2)], place, depth, scatter_sem)
        return carry

    lax.fori_loop(0, PLANE, scatter, 0)
    lax.fori_loop(1, PLANE, scatter_plane, 0)
    held[pl.ds(2 * spot, 2)] = tails[spot]

    attend_group(GROUPS - 1)

    late = jnp.exp2(new_scores[...] - top[:, :TOKENS])
    whole = norm[...] + jnp.sum(late, axis=1, keepdims=True)
    context = acc[...] + jnp.dot(
        late.astype(BF16), newest[:, HEAD_DIM:], preferred_element_type=F32
    )
    context = (context / whole).astype(BF16)
    context = jnp.dot(regroup[...], context, preferred_element_type=F32).astype(BF16)
    context = jnp.concatenate(
        [context[h * TOKENS : (h + 1) * TOKENS] for h in range(HEADS)], axis=1
    )

    wide_sends = []

    def project(k):
        weight_loads[k].wait()
        partial = jnp.dot(context, weight[k], preferred_element_type=F32)
        if k < 3:
            wide_out[k] = partial.astype(BF16)
            copy = pltpu.make_async_remote_copy(
                src_ref=wide_out.at[k],
                dst_ref=wide_in.at[k],
                send_sem=wide_send_sem.at[k],
                recv_sem=wide_recv_sem.at[k],
                device_id={"tp": lax.rem(column + 1 + k, 4) * 2 + side},
            )
            copy.start()
            wide_sends.append(copy)
        else:
            wide_own[...] = partial

    for k in range(4):
        project(k)

    wait_bytes(held.at[pl.ds(0, 4 * PLANE - 2)], scatter_sem.at[1])
    for place in range(PLANE):
        row = device(place, above)
        upward[place] = held[meta[row, 2 * MOVING + lane]]
        row = device(place, below)
        downward[place] = held[meta[row, 3 * MOVING + lane]]
        row = device(place, depth)
        inside[place, 0] = held[meta[row, lane]]
        inside[place, 1] = held[meta[row, MOVING + lane]]

    def forward(o, carry):
        place = lax.rem(spot + o, PLANE)
        send(upward.at[place], arrived.at[4 * spot + 2], place, above, forward_sem)
        send(downward.at[place], arrived.at[4 * spot + 3], place, below, forward_sem)
        return carry

    def forward_plane(o, carry):
        place = lax.rem(spot + o, PLANE)
        send(inside.at[place], arrived.at[pl.ds(4 * spot, 2)], place, depth, forward_sem)
        return carry

    lax.fori_loop(0, PLANE, forward, 0)
    lax.fori_loop(1, PLANE, forward_plane, 0)
    arrived[pl.ds(4 * spot, 2)] = inside[spot]

    for k in range(3):
        pltpu.make_async_copy(wide_in.at[k], wide_in.at[k], wide_recv_sem.at[k]).wait()
    total = wide_own[...]
    for k in range(3):
        total = total + wide_in[k].astype(F32)
    left, right = total[:, :NARROW], total[:, NARROW:]
    narrow_out[...] = jnp.where(side == 0, right, left).astype(BF16)
    narrow_send = pltpu.make_async_remote_copy(
        src_ref=narrow_out,
        dst_ref=narrow_in,
        send_sem=narrow_sem.at[0],
        recv_sem=narrow_sem.at[1],
        device_id={"tp": column * 2 + 1 - side},
    )
    narrow_send.start()
    own = jnp.where(side == 0, left, right)
    narrow_send.wait_recv()
    attended[...] = (own + narrow_in[...].astype(F32)).astype(BF16)

    landing_load.wait()

    wait_bytes(arrived.at[pl.ds(0, 4 * PLANE - 2)], forward_sem.at[1])

    land_rows = iota((LAND_ROWS, LANE_ROWS), 0)
    land_cols = iota((LAND_ROWS, LANE_ROWS), 1)
    target_rows = iota((LAND_ROWS, 2 * HEAD_DIM), 0)
    for m in range(MOVING):
        first = copied[0, m]
        total_in = meta[me, 4 * MOVING + m]
        rows = jnp.concatenate(
            [
                jnp.concatenate(
                    [
                        arrived[(2 * m + c) * 4 + meta[me, (5 + n) * MOVING + m]]
                        for c in range(2)
                    ],
                    axis=1,
                )
                for n in range(2)
            ],
            axis=0,
        )
        place = (land_rows - land_cols == first).astype(F32).astype(BF16)
        placed = jnp.dot(place, rows, preferred_element_type=F32).astype(BF16)
        fits = (target_rows >= first) & (target_rows < first + total_in)
        landed[m] = jnp.where(fits, placed, landing[m])

    for copy in wide_sends:
        copy.wait_send()
    narrow_send.wait_send()
    wait_bytes(held.at[pl.ds(0, 4 * PLANE - 2)], scatter_sem.at[0])
    wait_bytes(arrived.at[pl.ds(0, 4 * PLANE - 2)], forward_sem.at[0])


def publish(attended, landed, attended_out, landed_out, sems):
    copies = [pltpu.make_async_copy(attended, attended_out, sems.at[MOVING])] + [
        pltpu.make_async_copy(landed.at[m], landed_out.at[m], sems.at[m])
        for m in range(MOVING)
    ]
    for copy in copies:
        copy.start()
    for copy in copies:
        copy.wait()


def on_device(
    queries,
    key_values,
    new_key_values,
    cache_lengths,
    output_weight,
    moving_requests,
    migration_plan,
    row_counts,
    copied_rows,
    landing,
):
    in_hbm = pl.BlockSpec(memory_space=pltpu.HBM)
    dma = pltpu.SemaphoreType.DMA
    attended, landed = pl.pallas_call(
        main_kernel,
        out_shape=(
            jax.ShapeDtypeStruct((TOKENS, NARROW), BF16),
            jax.ShapeDtypeStruct((MOVING, LAND_ROWS, 2 * HEAD_DIM), BF16),
        ),
        in_specs=[in_hbm] * 10,
        out_specs=(
            pl.BlockSpec(memory_space=pltpu.VMEM),
            pl.BlockSpec(memory_space=pltpu.VMEM),
        ),
        scratch_shapes=[
            pltpu.SMEM((REQS,), I32),
            pltpu.SMEM((1, MOVING), I32),
            pltpu.SMEM((1, MOVING), I32),
            pltpu.VMEM((STEPS, REQS, HEADS * HEAD_DIM), BF16),
            pltpu.VMEM((TOKENS, 2 * HEAD_DIM), BF16),
            pltpu.VMEM((REQS * TILES, TILE, 2 * HEAD_DIM), BF16),
            pltpu.VMEM((4, HEADS * HEAD_DIM, WIDE), BF16),
            pltpu.VMEM((MOVING, INSTS), I32),
            pltpu.VMEM((STEPS, MOVING, INSTS), I32),
            pltpu.VMEM((MOVING, LAND_ROWS, 2 * HEAD_DIM), BF16),
            pltpu.VMEM((40, 128), I32),
            pltpu.SMEM((40, 128), I32),
            pltpu.VMEM((REQS * ROWS, HEAD_DIM), F32),
            pltpu.VMEM((REQS * ROWS, REQS * ROWS), BF16),
            pltpu.VMEM((REQS * ROWS, TOKENS), F32),
            pltpu.VMEM((REQS * ROWS, HEAD_DIM), F32),
            pltpu.VMEM((REQS * ROWS, HEAD_DIM), F32),
            pltpu.VMEM((REQS * ROWS, HEAD_DIM), F32),
            pltpu.VMEM((PLANE, 2, HALF, HEAD_DIM), BF16),
            pltpu.VMEM((4 * PLANE, HALF, HEAD_DIM), BF16),
            pltpu.VMEM((PLANE, 2, HALF, HEAD_DIM), BF16),
            pltpu.VMEM((PLANE, HALF, HEAD_DIM), BF16),
            pltpu.VMEM((PLANE, HALF, HEAD_DIM), BF16),
            pltpu.VMEM((4 * PLANE, HALF, HEAD_DIM), BF16),
            pltpu.VMEM((3, TOKENS, WIDE), BF16),
            pltpu.VMEM((3, TOKENS, WIDE), BF16),
            pltpu.VMEM((TOKENS, WIDE), F32),
            pltpu.VMEM((TOKENS, NARROW), BF16),
            pltpu.VMEM((TOKENS, NARROW), BF16),
            dma((7,)),
            dma((GROUPS,)),
            dma((4,)),
            dma((1,)),
            dma((1,)),
            dma((2,)),
            dma((2,)),
            dma((3,)),
            dma((3,)),
            dma((2,)),
        ],
        compiler_params=pltpu.CompilerParams(
            collective_id=0,
            has_side_effects=True,
            vmem_limit_bytes=40 * 1024 * 1024,
        ),
    )(
        *(
            pltpu.with_memory_space_constraint(x, pltpu.HBM)
            for x in (
                cache_lengths,
                moving_requests,
                copied_rows,
                queries,
                new_key_values.reshape(TOKENS, 2 * HEAD_DIM),
                key_values.reshape(REQS * TILES, TILE, 2 * HEAD_DIM),
                output_weight,
                migration_plan.T,
                row_counts.transpose(0, 2, 1),
                landing[0],
            )
        )
    )
    in_vmem = pl.BlockSpec(memory_space=pltpu.VMEM)
    anywhere = pl.BlockSpec(memory_space=pl.ANY)
    attended, landed = pl.pallas_call(
        publish,
        out_shape=(
            jax.ShapeDtypeStruct(attended.shape, BF16),
            jax.ShapeDtypeStruct(landed.shape, BF16),
        ),
        in_specs=[in_vmem, in_vmem],
        out_specs=(anywhere, anywhere),
        scratch_shapes=[dma((MOVING + 1,))],
        compiler_params=pltpu.CompilerParams(vmem_limit_bytes=4 * 1024 * 1024),
    )(
        pltpu.with_memory_space_constraint(attended, pltpu.VMEM),
        pltpu.with_memory_space_constraint(landed, pltpu.VMEM),
    )
    return attended.reshape(STEPS, REQS, NARROW), landed[None]


def solution(mesh):
    placed = (
        P(None, "inst", "tp"),
        P("inst", None, "tp"),
        P(None, "inst", "tp"),
        P("inst"),
        P("tp", None),
        P("inst", None),
        P(),
        P(),
        P("inst", None),
        P("inst", None, None, "tp"),
    )
    return jax.shard_map(
        on_device,
        mesh=mesh,
        in_specs=placed,
        out_specs=(P(None, "inst", "tp"), P("inst", None, None, "tp")),
        check_vma=False,
    )
```

```python
import functools
import math

import jax
import jax.numpy as jnp
from jax import lax
from jax.experimental import pallas as pl
from jax.experimental.pallas import tpu as pltpu
from jax.sharding import PartitionSpec as P

HEAD_DIM = 128
STEPS = 3
HEADS = 8
REQS = 16
CACHE = 1024
MOVING = 4
MOST_ROWS = 32
LANE_ROWS = STEPS * MOST_ROWS
LAND_ROWS = 256
INSTS = 32
PLANE = 8
HALF = LANE_ROWS // 2
BATCHES = HALF // 16
TP = 8
OUT_WIDTH = 4096
ROWS = STEPS * HEADS
TOKENS = STEPS * REQS
WIDE = OUT_WIDTH // 4
NARROW = OUT_WIDTH // TP
GROUP = 4
GROUPS = REQS // GROUP
TILE = 16
TILES = CACHE // TILE
WINDOW = LANE_ROWS + TILE
LOW = -1e30
SCALE = math.log2(math.e) / math.sqrt(HEAD_DIM)
F32 = jnp.float32
BF16 = jnp.bfloat16
I32 = jnp.int32


def iota(shape, dim):
    return lax.broadcasted_iota(I32, shape, dim)


def wait_bytes(ref, sem):
    pltpu.make_async_copy(ref, ref, sem).wait()


def main_kernel(
    lengths_hbm,
    moving_hbm,
    copied_hbm,
    queries_hbm,
    newest_hbm,
    cache_hbm,
    weight_hbm,
    plan_hbm,
    counts_hbm,
    landing_hbm,
    attended,
    landed,
    lengths,
    moving,
    copied,
    queries,
    newest,
    cache,
    weight,
    plan,
    counts,
    landing,
    meta_vec,
    meta,
    ordered,
    regroup,
    new_scores,
    acc,
    shifts,
    places,
    tails,
    held_0,
    held_1,
    held_2,
    inside,
    upward,
    downward,
    arrived,
    wide_out,
    wide_in,
    wide_own,
    narrow_out,
    narrow_in,
    small_sem,
    cache_sem,
    weight_sem,
    landing_sem,
    meta_sem,
    scatter_sem,
    forward_sem,
    wide_send_sem,
    wide_recv_sem,
    narrow_sem,
):
    me = lax.axis_index("inst")
    tp = lax.axis_index("tp")
    depth = lax.rem(me // 2, 4)
    spot = (me // 8) * 2 + lax.rem(me, 2)
    lane = me // 8
    column = tp // 2
    side = lax.rem(tp, 2)

    def device(place, plane):
        return ((place // 2) * 4 + plane) * 2 + lax.rem(place, 2)

    above, below = lax.rem(depth + 1, 4), lax.rem(depth + 3, 4)
    held = (held_0, held_1, held_2)

    barrier = pltpu.get_barrier_semaphore()

    def greet(o, carry):
        place = lax.rem(spot + o, PLANE)
        for plane in (above, below):
            pl.semaphore_signal(
                barrier, inc=1, device_id={"inst": device(place, plane)}
            )
        return carry

    def greet_plane(o, carry):
        place = lax.rem(spot + o, PLANE)
        pl.semaphore_signal(barrier, inc=1, device_id={"inst": device(place, depth)})
        return carry

    lax.fori_loop(0, PLANE, greet, 0)
    lax.fori_loop(1, PLANE, greet_plane, 0)
    for k in range(3):
        other = lax.rem(column + 1 + k, 4)
        pl.semaphore_signal(barrier, inc=1, device_id={"tp": other * 2 + side})
    pl.semaphore_signal(barrier, inc=1, device_id={"tp": column * 2 + 1 - side})

    small = [
        pltpu.make_async_copy(src, dst, small_sem.at[n])
        for n, (src, dst) in enumerate(
            [
                (queries_hbm, queries),
                (newest_hbm, newest),
                (plan_hbm, plan),
                (counts_hbm, counts),
                (lengths_hbm, lengths),
                (moving_hbm, moving),
                (copied_hbm, copied),
            ]
        )
    ]
    for copy in small:
        copy.start()
    cache_loads = []
    for g in range(GROUPS):
        part = pl.ds(g * GROUP * TILES, GROUP * TILES)
        cache_loads.append(
            pltpu.make_async_copy(cache_hbm.at[part], cache.at[part], cache_sem.at[g])
        )
        cache_loads[-1].start()
    weight_loads = []
    for k in range(4):
        target = lax.rem(column + 1 + k, 4)
        weight_loads.append(
            pltpu.make_async_copy(
                weight_hbm.at[:, pl.ds(pl.multiple_of(target * WIDE, WIDE), WIDE)],
                weight.at[k],
                weight_sem.at[k],
            )
        )
    landing_load = pltpu.make_async_copy(landing_hbm, landing, landing_sem.at[0])

    for copy in small:
        copy.wait()
    inst_rows = iota((INSTS, INSTS), 0)
    inst_cols = iota((INSTS, INSTS), 1)
    total = counts[0] + counts[1] + counts[2]
    for m in range(MOVING):
        hit = plan[m : m + 1, :] == inst_rows
        sender = jnp.sum(jnp.where(hit, inst_cols, 0), axis=1, keepdims=True)
        sender = jnp.minimum(sender, INSTS - 1)
        place = ((sender >> 3) << 1) + (sender & 1)
        plane = (sender >> 1) & 3
        offset = (plane - depth) & 3
        away = (plane - ((inst_rows[:, :1] >> 1) & 3)) & 3
        low, high = 2 * place, 2 * place + 1
        from_below, from_above = 2 * PLANE + place, 3 * PLANE + place
        columns = (
            jnp.where(offset == 3, from_below, low),
            jnp.where(offset == 1, from_above, high),
            jnp.where(offset == 3, from_below, high),
            jnp.where(offset == 1, from_above, low),
            jnp.sum(jnp.where(hit, total[m : m + 1, :], 0), axis=1, keepdims=True),
            jnp.where(away == 1, 3, jnp.where(away == 2, 2, 0)),
            jnp.where(away == 3, 2, jnp.where(away == 2, 3, 1)),
        )
        for n, values in enumerate(columns):
            n = n * MOVING + m
            meta_vec[0:INSTS, n : n + 1] = values
    meta_vec[INSTS : INSTS + MOVING, 0:INSTS] = total
    meta_load = pltpu.make_async_copy(meta_vec, meta, meta_sem.at[0])
    meta_load.start()

    stacked = jnp.concatenate(
        [
            queries[s, :, h * HEAD_DIM : (h + 1) * HEAD_DIM]
            for s in range(STEPS)
            for h in range(HEADS)
        ],
        axis=0,
    )
    pick = iota((ROWS, REQS * ROWS), 1) - REQS * iota((ROWS, REQS * ROWS), 0)
    order = jnp.concatenate(
        [(pick == b).astype(F32) for b in range(REQS)], axis=0
    ).astype(BF16)
    ordered[...] = jnp.dot(order, stacked, preferred_element_type=F32)
    back = iota((REQS, REQS * ROWS), 1) - ROWS * iota((REQS, REQS * ROWS), 0)
    for h in range(HEADS):
        for s in range(STEPS):
            n = (h * STEPS + s) * REQS
            regroup[n : n + REQS, :] = (back == s * HEADS + h).astype(F32).astype(BF16)
    fresh = lax.dot_general(
        ordered[...].astype(BF16),
        newest[:, :HEAD_DIM],
        (((1,), (1,)), ((), ())),
        preferred_element_type=F32,
    )
    position = iota((ROWS, TOKENS), 1)
    causal = (position >> 4) <= (iota((ROWS, TOKENS), 0) >> 3)
    for b in range(REQS):
        rows = slice(b * ROWS, (b + 1) * ROWS)
        valid = causal & ((position & (REQS - 1)) == b)
        new_scores[rows, :] = jnp.where(valid, fresh[rows] * SCALE, LOW)

    def attend_group(g):
        members = range(g * GROUP, (g + 1) * GROUP)
        rows = [slice(b * ROWS, (b + 1) * ROWS) for b in members]
        stored = [
            cache[b * TILES : (b + 1) * TILES].reshape(CACHE, 2 * HEAD_DIM) for b in members
        ]
        scores = [
            lax.dot_general(
                ordered[r, :].astype(BF16),
                kv[:, :HEAD_DIM],
                (((1,), (1,)), ((), ())),
                preferred_element_type=F32,
            )
            for r, kv in zip(rows, stored)
        ]
        scores = [
            jnp.where(iota((ROWS, CACHE), 1) < lengths[b], x * SCALE, LOW)
            for b, x in zip(members, scores)
        ]
        highest = [
            jnp.maximum(
                jnp.max(x, axis=1, keepdims=True),
                jnp.max(new_scores[r, :], axis=1, keepdims=True),
            )
            for r, x in zip(rows, scores)
        ]
        weights = [jnp.exp2(x - h) for x, h in zip(scores, highest)]
        late = [jnp.exp2(new_scores[r, :] - h) for r, h in zip(rows, highest)]
        shares = [
            1.0 / (jnp.sum(w, axis=1, keepdims=True) + jnp.sum(n, axis=1, keepdims=True))
            for w, n in zip(weights, late)
        ]
        outs = [
            jnp.dot((w * x).astype(BF16), kv[:, HEAD_DIM:], preferred_element_type=F32)
            for w, x, kv in zip(weights, shares, stored)
        ]
        for r, n, x, o in zip(rows, late, shares, outs):
            new_scores[r, :] = n * x
            acc[r, :] = o

    meta_load.wait()
    tail_rows = iota((LANE_ROWS, WINDOW), 0)
    tail_cols = iota((LANE_ROWS, WINDOW), 1)
    first_tiles = []
    for m in range(MOVING):
        total = meta[INSTS + m, me]
        start = lengths[moving[0, m]] - total
        first = jnp.minimum(start // TILE, TILES - WINDOW // TILE)
        first_tiles.append(first)
        shift = (tail_cols - tail_rows == start - first * TILE) & (tail_rows < total)
        shifts[m] = shift.astype(F32).astype(BF16)

    for g in range(GROUPS - 1):
        cache_loads[g].wait()
        if g == 1:
            for load in weight_loads:
                load.start()
            landing_load.start()
        attend_group(g)
    cache_loads[GROUPS - 1].wait()

    for m in range(MOVING):
        tile = moving[0, m] * TILES + first_tiles[m]
        window = jnp.concatenate(
            [cache[tile + t] for t in range(WINDOW // TILE)], axis=0
        )
        tail = jnp.dot(shifts[m], window, preferred_element_type=F32).astype(BF16)
        for c in range(2):
            for n in range(2):
                for t in range(BATCHES):
                    first_row = n * HALF + t * TILE
                    tails[t, 2 * m + c, n] = tail[
                        first_row : first_row + TILE, c * HEAD_DIM : (c + 1) * HEAD_DIM
                    ]

    pl.semaphore_wait(barrier, 3 * PLANE - 1 + 3 + 1)

    def send(src, dst, place, plane, sems, t):
        pltpu.make_async_remote_copy(
            src_ref=src,
            dst_ref=dst,
            send_sem=sems.at[0, t],
            recv_sem=sems.at[1, t],
            device_id={"inst": device(place, plane)},
        ).start()

    def scatter(t):
        def beside(o, carry):
            place = lax.rem(spot + o, PLANE)
            send(
                tails.at[t, place, 0],
                held[t].at[2 * PLANE + spot],
                place,
                above,
                scatter_sem,
                t,
            )
            send(
                tails.at[t, place, 1],
                held[t].at[3 * PLANE + spot],
                place,
                below,
                scatter_sem,
                t,
            )
            return carry

        def within(o, carry):
            place = lax.rem(spot + o, PLANE)
            send(
                tails.at[t, place],
                held[t].at[pl.ds(2 * spot, 2)],
                place,
                depth,
                scatter_sem,
                t,
            )
            return carry

        lax.fori_loop(0, PLANE, beside, 0)
        lax.fori_loop(1, PLANE, within, 0)
        held[t][pl.ds(2 * spot, 2)] = tails[t, spot]

    for t in range(BATCHES):
        scatter(t)

    attend_group(GROUPS - 1)

    context = acc[...] + jnp.dot(
        new_scores[...].astype(BF16), newest[:, HEAD_DIM:], preferred_element_type=F32
    )
    context = context.astype(BF16)
    context = jnp.dot(regroup[...], context, preferred_element_type=F32).astype(BF16)
    context = jnp.concatenate(
        [context[h * TOKENS : (h + 1) * TOKENS] for h in range(HEADS)], axis=1
    )

    wide_sends = []

    def project(k):
        weight_loads[k].wait()
        partial = jnp.dot(context, weight[k], preferred_element_type=F32)
        if k < 3:
            wide_out[k] = partial.astype(BF16)
            copy = pltpu.make_async_remote_copy(
                src_ref=wide_out.at[k],
                dst_ref=wide_in.at[k],
                send_sem=wide_send_sem.at[k],
                recv_sem=wide_recv_sem.at[k],
                device_id={"tp": lax.rem(column + 1 + k, 4) * 2 + side},
            )
            copy.start()
            wide_sends.append(copy)
        else:
            wide_own[...] = partial

    for k in range(4):
        project(k)

    land_rows = iota((LAND_ROWS, LANE_ROWS), 0)
    land_cols = iota((LAND_ROWS, LANE_ROWS), 1)
    target_rows = iota((LAND_ROWS, 2 * HEAD_DIM), 0)
    landing_load.wait()
    for m in range(MOVING):
        first = copied[0, m]
        total_in = meta[me, 4 * MOVING + m]
        place = (land_rows - land_cols == first) & (land_cols < total_in)
        places[m] = place.astype(F32).astype(BF16)
        fits = (target_rows >= first) & (target_rows < first + total_in)
        landing[m] = jnp.where(fits, 0.0, landing[m].astype(F32)).astype(BF16)

    def forward(t):
        wait_bytes(held[t].at[pl.ds(0, 4 * PLANE - 2)], scatter_sem.at[1, t])
        for place in range(PLANE):
            row = device(place, above)
            upward[t, place] = held[t][meta[row, 2 * MOVING + lane]]
            row = device(place, below)
            downward[t, place] = held[t][meta[row, 3 * MOVING + lane]]
            row = device(place, depth)
            inside[t, place, 0] = held[t][meta[row, lane]]
            inside[t, place, 1] = held[t][meta[row, MOVING + lane]]

        def beside(o, carry):
            place = lax.rem(spot + o, PLANE)
            send(
                upward.at[t, place],
                arrived.at[t, 4 * spot + 2],
                place,
                above,
                forward_sem,
                t,
            )
            send(
                downward.at[t, place],
                arrived.at[t, 4 * spot + 3],
                place,
                below,
                forward_sem,
                t,
            )
            return carry

        def within(o, carry):
            place = lax.rem(spot + o, PLANE)
            send(
                inside.at[t, place],
                arrived.at[t, pl.ds(4 * spot, 2)],
                place,
                depth,
                forward_sem,
                t,
            )
            return carry

        lax.fori_loop(0, PLANE, beside, 0)
        lax.fori_loop(1, PLANE, within, 0)
        arrived[t, pl.ds(4 * spot, 2)] = inside[t, spot]

    for t in range(BATCHES):
        forward(t)

    for k in range(3):
        pltpu.make_async_copy(wide_in.at[k], wide_in.at[k], wide_recv_sem.at[k]).wait()
    total = wide_own[...]
    for k in range(3):
        total = total + wide_in[k].astype(F32)
    left, right = total[:, :NARROW], total[:, NARROW:]
    narrow_out[...] = jnp.where(side == 0, right, left).astype(BF16)
    narrow_send = pltpu.make_async_remote_copy(
        src_ref=narrow_out,
        dst_ref=narrow_in,
        send_sem=narrow_sem.at[0],
        recv_sem=narrow_sem.at[1],
        device_id={"tp": column * 2 + 1 - side},
    )
    narrow_send.start()
    own = jnp.where(side == 0, left, right)
    narrow_send.wait_recv()
    attended[...] = (own + narrow_in[...].astype(F32)).astype(BF16)

    for t in range(BATCHES):
        wait_bytes(arrived.at[t, pl.ds(0, 4 * PLANE - 2)], forward_sem.at[1, t])

    for m in range(MOVING):
        rows = jnp.concatenate(
            [
                jnp.concatenate(
                    [
                        arrived[t, (2 * m + c) * 4 + meta[me, (5 + n) * MOVING + m]]
                        for c in range(2)
                    ],
                    axis=1,
                )
                for n in range(2)
                for t in range(BATCHES)
            ],
            axis=0,
        )
        placed = jnp.dot(places[m], rows, preferred_element_type=F32)
        landed[m] = (landing[m].astype(F32) + placed).astype(BF16)

    for copy in wide_sends:
        copy.wait_send()
    narrow_send.wait_send()
    for t in range(BATCHES):
        wait_bytes(held[t].at[pl.ds(0, 4 * PLANE - 2)], scatter_sem.at[0, t])
        wait_bytes(arrived.at[t, pl.ds(0, 4 * PLANE - 2)], forward_sem.at[0, t])


def publish(attended, landed, attended_out, landed_out, sems):
    copies = [pltpu.make_async_copy(attended, attended_out, sems.at[MOVING])] + [
        pltpu.make_async_copy(landed.at[m], landed_out.at[m], sems.at[m])
        for m in range(MOVING)
    ]
    for copy in copies:
        copy.start()
    for copy in copies:
        copy.wait()


def on_device(
    queries,
    key_values,
    new_key_values,
    cache_lengths,
    output_weight,
    moving_requests,
    migration_plan,
    row_counts,
    copied_rows,
    landing,
):
    in_hbm = pl.BlockSpec(memory_space=pltpu.HBM)
    dma = pltpu.SemaphoreType.DMA
    attended, landed = pl.pallas_call(
        main_kernel,
        out_shape=(
            jax.ShapeDtypeStruct((TOKENS, NARROW), BF16),
            jax.ShapeDtypeStruct((MOVING, LAND_ROWS, 2 * HEAD_DIM), BF16),
        ),
        in_specs=[in_hbm] * 10,
        out_specs=(
            pl.BlockSpec(memory_space=pltpu.VMEM),
            pl.BlockSpec(memory_space=pltpu.VMEM),
        ),
        scratch_shapes=[
            pltpu.SMEM((REQS,), I32),
            pltpu.SMEM((1, MOVING), I32),
            pltpu.SMEM((1, MOVING), I32),
            pltpu.VMEM((STEPS, REQS, HEADS * HEAD_DIM), BF16),
            pltpu.VMEM((TOKENS, 2 * HEAD_DIM), BF16),
            pltpu.VMEM((REQS * TILES, TILE, 2 * HEAD_DIM), BF16),
            pltpu.VMEM((4, HEADS * HEAD_DIM, WIDE), BF16),
            pltpu.VMEM((MOVING, INSTS), I32),
            pltpu.VMEM((STEPS, MOVING, INSTS), I32),
            pltpu.VMEM((MOVING, LAND_ROWS, 2 * HEAD_DIM), BF16),
            pltpu.VMEM((40, 128), I32),
            pltpu.SMEM((40, 128), I32),
            pltpu.VMEM((REQS * ROWS, HEAD_DIM), F32),
            pltpu.VMEM((REQS * ROWS, REQS * ROWS), BF16),
            pltpu.VMEM((REQS * ROWS, TOKENS), F32),
            pltpu.VMEM((REQS * ROWS, HEAD_DIM), F32),
            pltpu.VMEM((MOVING, LANE_ROWS, WINDOW), BF16),
            pltpu.VMEM((MOVING, LAND_ROWS, LANE_ROWS), BF16),
            pltpu.VMEM((BATCHES, PLANE, 2, TILE, HEAD_DIM), BF16),
            pltpu.VMEM((4 * PLANE, TILE, HEAD_DIM), BF16),
            pltpu.VMEM((4 * PLANE, TILE, HEAD_DIM), BF16),
            pltpu.VMEM((4 * PLANE, TILE, HEAD_DIM), BF16),
            pltpu.VMEM((BATCHES, PLANE, 2, TILE, HEAD_DIM), BF16),
            pltpu.VMEM((BATCHES, PLANE, TILE, HEAD_DIM), BF16),
            pltpu.VMEM((BATCHES, PLANE, TILE, HEAD_DIM), BF16),
            pltpu.VMEM((BATCHES, 4 * PLANE, TILE, HEAD_DIM), BF16),
            pltpu.VMEM((3, TOKENS, WIDE), BF16),
            pltpu.VMEM((3, TOKENS, WIDE), BF16),
            pltpu.VMEM((TOKENS, WIDE), F32),
            pltpu.VMEM((TOKENS, NARROW), BF16),
            pltpu.VMEM((TOKENS, NARROW), BF16),
            dma((7,)),
            dma((GROUPS,)),
            dma((4,)),
            dma((1,)),
            dma((1,)),
            dma((2, BATCHES)),
            dma((2, BATCHES)),
            dma((3,)),
            dma((3,)),
            dma((2,)),
        ],
        compiler_params=pltpu.CompilerParams(
            collective_id=0,
            has_side_effects=True,
            vmem_limit_bytes=40 * 1024 * 1024,
        ),
    )(
        *(
            pltpu.with_memory_space_constraint(x, pltpu.HBM)
            for x in (
                cache_lengths,
                moving_requests,
                copied_rows,
                queries,
                new_key_values.reshape(TOKENS, 2 * HEAD_DIM),
                key_values.reshape(REQS * TILES, TILE, 2 * HEAD_DIM),
                output_weight,
                migration_plan.T,
                row_counts.transpose(0, 2, 1),
                landing[0],
            )
        )
    )
    in_vmem = pl.BlockSpec(memory_space=pltpu.VMEM)
    anywhere = pl.BlockSpec(memory_space=pl.ANY)
    attended, landed = pl.pallas_call(
        publish,
        out_shape=(
            jax.ShapeDtypeStruct(attended.shape, BF16),
            jax.ShapeDtypeStruct(landed.shape, BF16),
        ),
        in_specs=[in_vmem, in_vmem],
        out_specs=(anywhere, anywhere),
        scratch_shapes=[dma((MOVING + 1,))],
        compiler_params=pltpu.CompilerParams(vmem_limit_bytes=4 * 1024 * 1024),
    )(
        pltpu.with_memory_space_constraint(attended, pltpu.VMEM),
        pltpu.with_memory_space_constraint(landed, pltpu.VMEM),
    )
    return attended.reshape(STEPS, REQS, NARROW), landed[None]


def solution(mesh):
    placed = (
        P(None, "inst", "tp"),
        P("inst", None, "tp"),
        P(None, "inst", "tp"),
        P("inst"),
        P("tp", None),
        P("inst", None),
        P(),
        P(),
        P("inst", None),
        P("inst", None, None, "tp"),
    )
    return jax.shard_map(
        on_device,
        mesh=mesh,
        in_specs=placed,
        out_specs=(P(None, "inst", "tp"), P("inst", None, None, "tp")),
        check_vma=False,
    )
```

```python
import functools
import math

import jax
import jax.numpy as jnp
from jax import lax
from jax.experimental import pallas as pl
from jax.experimental.pallas import tpu as pltpu
from jax.sharding import PartitionSpec as P

HEAD_DIM = 128
STEPS = 3
HEADS = 8
REQS = 16
CACHE = 1024
MOVING = 4
MOST_ROWS = 32
LANE_ROWS = STEPS * MOST_ROWS
LAND_ROWS = 256
INSTS = 32
PLANE = 8
HALF = LANE_ROWS // 2
BATCHES = HALF // 16
TP = 8
OUT_WIDTH = 4096
ROWS = STEPS * HEADS
TOKENS = STEPS * REQS
WIDE = OUT_WIDTH // 4
NARROW = OUT_WIDTH // TP
GROUP = 4
GROUPS = REQS // GROUP
TILE = 16
TILES = CACHE // TILE
WINDOW = LANE_ROWS + TILE
LOW = -1e30
SCALE = math.log2(math.e) / math.sqrt(HEAD_DIM)
F32 = jnp.float32
BF16 = jnp.bfloat16
I32 = jnp.int32


def iota(shape, dim):
    return lax.broadcasted_iota(I32, shape, dim)


def wait_bytes(ref, sem):
    pltpu.make_async_copy(ref, ref, sem).wait()


def main_kernel(
    lengths_hbm,
    moving_hbm,
    copied_hbm,
    queries_hbm,
    newest_hbm,
    cache_hbm,
    weight_hbm,
    plan_hbm,
    counts_hbm,
    landing_hbm,
    attended,
    landed,
    lengths,
    moving,
    copied,
    queries,
    newest,
    cache,
    weight,
    plan,
    counts,
    landing,
    meta_vec,
    meta,
    ordered,
    regroup,
    new_scores,
    acc,
    shifts,
    places,
    tails,
    held_0,
    held_1,
    held_2,
    inside,
    upward,
    downward,
    arrived,
    wide_out,
    wide_in,
    wide_own,
    narrow_out,
    narrow_in,
    small_sem,
    cache_sem,
    weight_sem,
    landing_sem,
    meta_sem,
    scatter_sem,
    forward_sem,
    wide_send_sem,
    wide_recv_sem,
    narrow_sem,
):
    me = lax.axis_index("inst")
    tp = lax.axis_index("tp")
    depth = lax.rem(me // 2, 4)
    spot = (me // 8) * 2 + lax.rem(me, 2)
    lane = me // 8
    column = tp // 2
    side = lax.rem(tp, 2)

    def device(place, plane):
        return ((place // 2) * 4 + plane) * 2 + lax.rem(place, 2)

    above, below = lax.rem(depth + 1, 4), lax.rem(depth + 3, 4)
    held = (held_0, held_1, held_2)

    barrier = pltpu.get_barrier_semaphore()

    def greet(o, carry):
        place = lax.rem(spot + o, PLANE)
        for plane in (above, below):
            pl.semaphore_signal(
                barrier, inc=1, device_id={"inst": device(place, plane)}
            )
        return carry

    def greet_plane(o, carry):
        place = lax.rem(spot + o, PLANE)
        pl.semaphore_signal(barrier, inc=1, device_id={"inst": device(place, depth)})
        return carry

    lax.fori_loop(0, PLANE, greet, 0)
    lax.fori_loop(1, PLANE, greet_plane, 0)
    for k in range(3):
        other = lax.rem(column + 1 + k, 4)
        pl.semaphore_signal(barrier, inc=1, device_id={"tp": other * 2 + side})
    pl.semaphore_signal(barrier, inc=1, device_id={"tp": column * 2 + 1 - side})

    small = [
        pltpu.make_async_copy(src, dst, small_sem.at[n])
        for n, (src, dst) in enumerate(
            [
                (queries_hbm, queries),
                (newest_hbm, newest),
                (plan_hbm, plan),
                (counts_hbm, counts),
                (lengths_hbm, lengths),
                (moving_hbm, moving),
                (copied_hbm, copied),
            ]
        )
    ]
    for copy in small:
        copy.start()
    cache_loads = []
    for g in range(GROUPS):
        part = pl.ds(g * GROUP * TILES, GROUP * TILES)
        cache_loads.append(
            pltpu.make_async_copy(cache_hbm.at[part], cache.at[part], cache_sem.at[g])
        )
        cache_loads[-1].start()
    weight_loads = []
    for k in range(4):
        target = lax.rem(column + 1 + k, 4)
        weight_loads.append(
            pltpu.make_async_copy(
                weight_hbm.at[:, pl.ds(pl.multiple_of(target * WIDE, WIDE), WIDE)],
                weight.at[k],
                weight_sem.at[k],
            )
        )
    landing_load = pltpu.make_async_copy(landing_hbm, landing, landing_sem.at[0])

    for copy in small:
        copy.wait()
    inst_rows = iota((INSTS, INSTS), 0)
    inst_cols = iota((INSTS, INSTS), 1)
    total = counts[0] + counts[1] + counts[2]
    for m in range(MOVING):
        hit = plan[m : m + 1, :] == inst_rows
        sender = jnp.sum(jnp.where(hit, inst_cols, 0), axis=1, keepdims=True)
        sender = jnp.minimum(sender, INSTS - 1)
        place = ((sender >> 3) << 1) + (sender & 1)
        plane = (sender >> 1) & 3
        offset = (plane - depth) & 3
        away = (plane - ((inst_rows[:, :1] >> 1) & 3)) & 3
        low, high = 2 * place, 2 * place + 1
        from_below, from_above = 2 * PLANE + place, 3 * PLANE + place
        columns = (
            jnp.where(offset == 3, from_below, low),
            jnp.where(offset == 1, from_above, high),
            jnp.where(offset == 3, from_below, high),
            jnp.where(offset == 1, from_above, low),
            jnp.sum(jnp.where(hit, total[m : m + 1, :], 0), axis=1, keepdims=True),
            jnp.where(away == 1, 3, jnp.where(away == 2, 2, 0)),
            jnp.where(away == 3, 2, jnp.where(away == 2, 3, 1)),
        )
        for n, values in enumerate(columns):
            n = n * MOVING + m
            meta_vec[0:INSTS, n : n + 1] = values
    meta_vec[INSTS : INSTS + MOVING, 0:INSTS] = total
    meta_load = pltpu.make_async_copy(meta_vec, meta, meta_sem.at[0])
    meta_load.start()

    stacked = jnp.concatenate(
        [
            queries[s, :, h * HEAD_DIM : (h + 1) * HEAD_DIM]
            for s in range(STEPS)
            for h in range(HEADS)
        ],
        axis=0,
    )
    pick = iota((ROWS, REQS * ROWS), 1) - REQS * iota((ROWS, REQS * ROWS), 0)
    order = jnp.concatenate(
        [(pick == b).astype(F32) for b in range(REQS)], axis=0
    ).astype(BF16)
    ordered[...] = jnp.dot(order, stacked, preferred_element_type=F32)
    back = iota((REQS, REQS * ROWS), 1) - ROWS * iota((REQS, REQS * ROWS), 0)
    for h in range(HEADS):
        for s in range(STEPS):
            n = (h * STEPS + s) * REQS
            regroup[n : n + REQS, :] = (back == s * HEADS + h).astype(F32).astype(BF16)
    fresh = lax.dot_general(
        ordered[...].astype(BF16),
        newest[:, :HEAD_DIM],
        (((1,), (1,)), ((), ())),
        preferred_element_type=F32,
    )
    position = iota((ROWS, TOKENS), 1)
    causal = (position >> 4) <= (iota((ROWS, TOKENS), 0) >> 3)
    for b in range(REQS):
        rows = slice(b * ROWS, (b + 1) * ROWS)
        valid = causal & ((position & (REQS - 1)) == b)
        new_scores[rows, :] = jnp.where(valid, fresh[rows] * SCALE, LOW)

    def attend_group(g):
        members = range(g * GROUP, (g + 1) * GROUP)
        rows = [slice(b * ROWS, (b + 1) * ROWS) for b in members]
        stored = [
            cache[b * TILES : (b + 1) * TILES].reshape(CACHE, 2 * HEAD_DIM) for b in members
        ]
        scores = [
            lax.dot_general(
                ordered[r, :].astype(BF16),
                kv[:, :HEAD_DIM],
                (((1,), (1,)), ((), ())),
                preferred_element_type=F32,
            )
            for r, kv in zip(rows, stored)
        ]
        scores = [
            jnp.where(iota((ROWS, CACHE), 1) < lengths[b], x * SCALE, LOW)
            for b, x in zip(members, scores)
        ]
        highest = [
            jnp.maximum(
                jnp.max(x, axis=1, keepdims=True),
                jnp.max(new_scores[r, :], axis=1, keepdims=True),
            )
            for r, x in zip(rows, scores)
        ]
        weights = [jnp.exp2(x - h) for x, h in zip(scores, highest)]
        late = [jnp.exp2(new_scores[r, :] - h) for r, h in zip(rows, highest)]
        shares = [
            1.0 / (jnp.sum(w, axis=1, keepdims=True) + jnp.sum(n, axis=1, keepdims=True))
            for w, n in zip(weights, late)
        ]
        outs = [
            jnp.dot((w * x).astype(BF16), kv[:, HEAD_DIM:], preferred_element_type=F32)
            for w, x, kv in zip(weights, shares, stored)
        ]
        for r, n, x, o in zip(rows, late, shares, outs):
            new_scores[r, :] = n * x
            acc[r, :] = o

    meta_load.wait()
    tail_rows = iota((LANE_ROWS, WINDOW), 0)
    tail_cols = iota((LANE_ROWS, WINDOW), 1)
    first_tiles = []
    for m in range(MOVING):
        total = meta[INSTS + m, me]
        start = lengths[moving[0, m]] - total
        first = jnp.minimum(start // TILE, TILES - WINDOW // TILE)
        first_tiles.append(first)
        shift = (tail_cols - tail_rows == start - first * TILE) & (tail_rows < total)
        shifts[m] = shift.astype(F32).astype(BF16)

    for g in range(1):
        cache_loads[g].wait()
        if g == 0:
            for load in weight_loads:
                load.start()
            landing_load.start()
        attend_group(g)
    for g in range(1, GROUPS):
        cache_loads[g].wait()

    for m in range(MOVING):
        tile = moving[0, m] * TILES + first_tiles[m]
        window = jnp.concatenate(
            [cache[tile + t] for t in range(WINDOW // TILE)], axis=0
        )
        tail = jnp.dot(shifts[m], window, preferred_element_type=F32).astype(BF16)
        for c in range(2):
            for n in range(2):
                for t in range(BATCHES):
                    first_row = n * HALF + t * TILE
                    tails[t, 2 * m + c, n] = tail[
                        first_row : first_row + TILE, c * HEAD_DIM : (c + 1) * HEAD_DIM
                    ]

    pl.semaphore_wait(barrier, 3 * PLANE - 1 + 3 + 1)

    def send(src, dst, place, plane, sems, t):
        pltpu.make_async_remote_copy(
            src_ref=src,
            dst_ref=dst,
            send_sem=sems.at[0, t],
            recv_sem=sems.at[1, t],
            device_id={"inst": device(place, plane)},
        ).start()

    def scatter(t):
        def beside(o, carry):
            place = lax.rem(spot + o, PLANE)
            send(
                tails.at[t, place, 0],
                held[t].at[2 * PLANE + spot],
                place,
                above,
                scatter_sem,
                t,
            )
            send(
                tails.at[t, place, 1],
                held[t].at[3 * PLANE + spot],
                place,
                below,
                scatter_sem,
                t,
            )
            return carry

        def within(o, carry):
            place = lax.rem(spot + o, PLANE)
            send(
                tails.at[t, place],
                held[t].at[pl.ds(2 * spot, 2)],
                place,
                depth,
                scatter_sem,
                t,
            )
            return carry

        lax.fori_loop(0, PLANE, beside, 0)
        lax.fori_loop(1, PLANE, within, 0)
        held[t][pl.ds(2 * spot, 2)] = tails[t, spot]

    for t in range(BATCHES):
        scatter(t)

    for g in range(1, GROUPS):
        attend_group(g)

    context = acc[...] + jnp.dot(
        new_scores[...].astype(BF16), newest[:, HEAD_DIM:], preferred_element_type=F32
    )
    context = context.astype(BF16)
    context = jnp.dot(regroup[...], context, preferred_element_type=F32).astype(BF16)
    context = jnp.concatenate(
        [context[h * TOKENS : (h + 1) * TOKENS] for h in range(HEADS)], axis=1
    )

    wide_sends = []

    def project(k):
        weight_loads[k].wait()
        partial = jnp.dot(context, weight[k], preferred_element_type=F32)
        if k < 3:
            wide_out[k] = partial.astype(BF16)
            copy = pltpu.make_async_remote_copy(
                src_ref=wide_out.at[k],
                dst_ref=wide_in.at[k],
                send_sem=wide_send_sem.at[k],
                recv_sem=wide_recv_sem.at[k],
                device_id={"tp": lax.rem(column + 1 + k, 4) * 2 + side},
            )
            copy.start()
            wide_sends.append(copy)
        else:
            wide_own[...] = partial

    for k in range(4):
        project(k)

    def forward(t):
        wait_bytes(held[t].at[pl.ds(0, 4 * PLANE - 2)], scatter_sem.at[1, t])
        for place in range(PLANE):
            row = device(place, above)
            upward[t, place] = held[t][meta[row, 2 * MOVING + lane]]
            row = device(place, below)
            downward[t, place] = held[t][meta[row, 3 * MOVING + lane]]
            row = device(place, depth)
            inside[t, place, 0] = held[t][meta[row, lane]]
            inside[t, place, 1] = held[t][meta[row, MOVING + lane]]

        def beside(o, carry):
            place = lax.rem(spot + o, PLANE)
            send(
                upward.at[t, place],
                arrived.at[t, 4 * spot + 2],
                place,
                above,
                forward_sem,
                t,
            )
            send(
                downward.at[t, place],
                arrived.at[t, 4 * spot + 3],
                place,
                below,
                forward_sem,
                t,
            )
            return carry

        def within(o, carry):
            place = lax.rem(spot + o, PLANE)
            send(
                inside.at[t, place],
                arrived.at[t, pl.ds(4 * spot, 2)],
                place,
                depth,
                forward_sem,
                t,
            )
            return carry

        lax.fori_loop(0, PLANE, beside, 0)
        lax.fori_loop(1, PLANE, within, 0)
        arrived[t, pl.ds(4 * spot, 2)] = inside[t, spot]

    for t in range(BATCHES):
        forward(t)

    land_rows = iota((LAND_ROWS, LANE_ROWS), 0)
    land_cols = iota((LAND_ROWS, LANE_ROWS), 1)
    target_rows = iota((LAND_ROWS, 2 * HEAD_DIM), 0)
    landing_load.wait()
    for m in range(MOVING):
        first = copied[0, m]
        total_in = meta[me, 4 * MOVING + m]
        place = (land_rows - land_cols == first) & (land_cols < total_in)
        places[m] = place.astype(F32).astype(BF16)
        fits = (target_rows >= first) & (target_rows < first + total_in)
        landing[m] = jnp.where(fits, 0.0, landing[m].astype(F32)).astype(BF16)

    for k in range(3):
        pltpu.make_async_copy(wide_in.at[k], wide_in.at[k], wide_recv_sem.at[k]).wait()
    total = wide_own[...]
    for k in range(3):
        total = total + wide_in[k].astype(F32)
    left, right = total[:, :NARROW], total[:, NARROW:]
    narrow_out[...] = jnp.where(side == 0, right, left).astype(BF16)
    narrow_send = pltpu.make_async_remote_copy(
        src_ref=narrow_out,
        dst_ref=narrow_in,
        send_sem=narrow_sem.at[0],
        recv_sem=narrow_sem.at[1],
        device_id={"tp": column * 2 + 1 - side},
    )
    narrow_send.start()
    own = jnp.where(side == 0, left, right)
    narrow_send.wait_recv()
    attended[...] = (own + narrow_in[...].astype(F32)).astype(BF16)

    for t in range(BATCHES):
        wait_bytes(arrived.at[t, pl.ds(0, 4 * PLANE - 2)], forward_sem.at[1, t])

    for m in range(MOVING):
        rows = jnp.concatenate(
            [
                jnp.concatenate(
                    [
                        arrived[t, (2 * m + c) * 4 + meta[me, (5 + n) * MOVING + m]]
                        for c in range(2)
                    ],
                    axis=1,
                )
                for n in range(2)
                for t in range(BATCHES)
            ],
            axis=0,
        )
        placed = jnp.dot(places[m], rows, preferred_element_type=F32)
        landed[m] = (landing[m].astype(F32) + placed).astype(BF16)

    for copy in wide_sends:
        copy.wait_send()
    narrow_send.wait_send()
    for t in range(BATCHES):
        wait_bytes(held[t].at[pl.ds(0, 4 * PLANE - 2)], scatter_sem.at[0, t])
        wait_bytes(arrived.at[t, pl.ds(0, 4 * PLANE - 2)], forward_sem.at[0, t])


def publish(attended, landed, attended_out, landed_out, sems):
    copies = [pltpu.make_async_copy(attended, attended_out, sems.at[MOVING])] + [
        pltpu.make_async_copy(landed.at[m], landed_out.at[m], sems.at[m])
        for m in range(MOVING)
    ]
    for copy in copies:
        copy.start()
    for copy in copies:
        copy.wait()


def on_device(
    queries,
    key_values,
    new_key_values,
    cache_lengths,
    output_weight,
    moving_requests,
    migration_plan,
    row_counts,
    copied_rows,
    landing,
):
    in_hbm = pl.BlockSpec(memory_space=pltpu.HBM)
    dma = pltpu.SemaphoreType.DMA
    attended, landed = pl.pallas_call(
        main_kernel,
        out_shape=(
            jax.ShapeDtypeStruct((TOKENS, NARROW), BF16),
            jax.ShapeDtypeStruct((MOVING, LAND_ROWS, 2 * HEAD_DIM), BF16),
        ),
        in_specs=[in_hbm] * 10,
        out_specs=(
            pl.BlockSpec(memory_space=pltpu.VMEM),
            pl.BlockSpec(memory_space=pltpu.VMEM),
        ),
        scratch_shapes=[
            pltpu.SMEM((REQS,), I32),
            pltpu.SMEM((1, MOVING), I32),
            pltpu.SMEM((1, MOVING), I32),
            pltpu.VMEM((STEPS, REQS, HEADS * HEAD_DIM), BF16),
            pltpu.VMEM((TOKENS, 2 * HEAD_DIM), BF16),
            pltpu.VMEM((REQS * TILES, TILE, 2 * HEAD_DIM), BF16),
            pltpu.VMEM((4, HEADS * HEAD_DIM, WIDE), BF16),
            pltpu.VMEM((MOVING, INSTS), I32),
            pltpu.VMEM((STEPS, MOVING, INSTS), I32),
            pltpu.VMEM((MOVING, LAND_ROWS, 2 * HEAD_DIM), BF16),
            pltpu.VMEM((40, 128), I32),
            pltpu.SMEM((40, 128), I32),
            pltpu.VMEM((REQS * ROWS, HEAD_DIM), F32),
            pltpu.VMEM((REQS * ROWS, REQS * ROWS), BF16),
            pltpu.VMEM((REQS * ROWS, TOKENS), F32),
            pltpu.VMEM((REQS * ROWS, HEAD_DIM), F32),
            pltpu.VMEM((MOVING, LANE_ROWS, WINDOW), BF16),
            pltpu.VMEM((MOVING, LAND_ROWS, LANE_ROWS), BF16),
            pltpu.VMEM((BATCHES, PLANE, 2, TILE, HEAD_DIM), BF16),
            pltpu.VMEM((4 * PLANE, TILE, HEAD_DIM), BF16),
            pltpu.VMEM((4 * PLANE, TILE, HEAD_DIM), BF16),
            pltpu.VMEM((4 * PLANE, TILE, HEAD_DIM), BF16),
            pltpu.VMEM((BATCHES, PLANE, 2, TILE, HEAD_DIM), BF16),
            pltpu.VMEM((BATCHES, PLANE, TILE, HEAD_DIM), BF16),
            pltpu.VMEM((BATCHES, PLANE, TILE, HEAD_DIM), BF16),
            pltpu.VMEM((BATCHES, 4 * PLANE, TILE, HEAD_DIM), BF16),
            pltpu.VMEM((3, TOKENS, WIDE), BF16),
            pltpu.VMEM((3, TOKENS, WIDE), BF16),
            pltpu.VMEM((TOKENS, WIDE), F32),
            pltpu.VMEM((TOKENS, NARROW), BF16),
            pltpu.VMEM((TOKENS, NARROW), BF16),
            dma((7,)),
            dma((GROUPS,)),
            dma((4,)),
            dma((1,)),
            dma((1,)),
            dma((2, BATCHES)),
            dma((2, BATCHES)),
            dma((3,)),
            dma((3,)),
            dma((2,)),
        ],
        compiler_params=pltpu.CompilerParams(
            collective_id=0,
            has_side_effects=True,
            vmem_limit_bytes=40 * 1024 * 1024,
        ),
    )(
        *(
            pltpu.with_memory_space_constraint(x, pltpu.HBM)
            for x in (
                cache_lengths,
                moving_requests,
                copied_rows,
                queries,
                new_key_values.reshape(TOKENS, 2 * HEAD_DIM),
                key_values.reshape(REQS * TILES, TILE, 2 * HEAD_DIM),
                output_weight,
                migration_plan.T,
                row_counts.transpose(0, 2, 1),
                landing[0],
            )
        )
    )
    in_vmem = pl.BlockSpec(memory_space=pltpu.VMEM)
    anywhere = pl.BlockSpec(memory_space=pl.ANY)
    attended, landed = pl.pallas_call(
        publish,
        out_shape=(
            jax.ShapeDtypeStruct(attended.shape, BF16),
            jax.ShapeDtypeStruct(landed.shape, BF16),
        ),
        in_specs=[in_vmem, in_vmem],
        out_specs=(anywhere, anywhere),
        scratch_shapes=[dma((MOVING + 1,))],
        compiler_params=pltpu.CompilerParams(vmem_limit_bytes=4 * 1024 * 1024),
    )(
        pltpu.with_memory_space_constraint(attended, pltpu.VMEM),
        pltpu.with_memory_space_constraint(landed, pltpu.VMEM),
    )
    return attended.reshape(STEPS, REQS, NARROW), landed[None]


def solution(mesh):
    placed = (
        P(None, "inst", "tp"),
        P("inst", None, "tp"),
        P(None, "inst", "tp"),
        P("inst"),
        P("tp", None),
        P("inst", None),
        P(),
        P(),
        P("inst", None),
        P("inst", None, None, "tp"),
    )
    return jax.shard_map(
        on_device,
        mesh=mesh,
        in_specs=placed,
        out_specs=(P(None, "inst", "tp"), P("inst", None, None, "tp")),
        check_vma=False,
    )
```

```python
import functools
import math

import jax
import jax.numpy as jnp
from jax import lax
from jax.experimental import pallas as pl
from jax.experimental.pallas import tpu as pltpu
from jax.sharding import PartitionSpec as P

HEAD_DIM = 128
STEPS = 3
HEADS = 8
REQS = 16
CACHE = 1024
MOVING = 4
MOST_ROWS = 32
LANE_ROWS = STEPS * MOST_ROWS
LAND_ROWS = 256
INSTS = 32
PLANE = 8
HALF = LANE_ROWS // 2
BATCHES = HALF // 16
TP = 8
OUT_WIDTH = 4096
ROWS = STEPS * HEADS
TOKENS = STEPS * REQS
WIDE = OUT_WIDTH // 4
NARROW = OUT_WIDTH // TP
GROUP = 4
GROUPS = REQS // GROUP
TILE = 16
TILES = CACHE // TILE
WINDOW = LANE_ROWS + TILE
LOW = -1e30
SCALE = math.log2(math.e) / math.sqrt(HEAD_DIM)
F32 = jnp.float32
BF16 = jnp.bfloat16
I32 = jnp.int32


def iota(shape, dim):
    return lax.broadcasted_iota(I32, shape, dim)


def wait_bytes(ref, sem):
    pltpu.make_async_copy(ref, ref, sem).wait()


def main_kernel(
    lengths_hbm,
    moving_hbm,
    copied_hbm,
    queries_hbm,
    newest_hbm,
    cache_hbm,
    weight_hbm,
    plan_hbm,
    counts_hbm,
    landing_hbm,
    attended,
    landed,
    lengths,
    moving,
    copied,
    queries,
    newest,
    cache,
    weight,
    plan,
    counts,
    landing,
    meta_vec,
    meta,
    ordered,
    regroup,
    new_scores,
    acc,
    shifts,
    places,
    tails,
    held_0,
    held_1,
    held_2,
    inside,
    upward,
    downward,
    arrived,
    wide_out,
    wide_in,
    wide_own,
    narrow_out,
    narrow_in,
    small_sem,
    cache_sem,
    weight_sem,
    landing_sem,
    meta_sem,
    scatter_sem,
    forward_sem,
    wide_send_sem,
    wide_recv_sem,
    narrow_sem,
):
    me = lax.axis_index("inst")
    tp = lax.axis_index("tp")
    depth = lax.rem(me // 2, 4)
    spot = (me // 8) * 2 + lax.rem(me, 2)
    lane = me // 8
    column = tp // 2
    side = lax.rem(tp, 2)

    def device(place, plane):
        return ((place // 2) * 4 + plane) * 2 + lax.rem(place, 2)

    above, below = lax.rem(depth + 1, 4), lax.rem(depth + 3, 4)
    held = (held_0, held_1, held_2)

    barrier = pltpu.get_barrier_semaphore()

    def greet(o, carry):
        place = lax.rem(spot + o, PLANE)
        for plane in (above, below):
            pl.semaphore_signal(
                barrier, inc=1, device_id={"inst": device(place, plane)}
            )
        return carry

    def greet_plane(o, carry):
        place = lax.rem(spot + o, PLANE)
        pl.semaphore_signal(barrier, inc=1, device_id={"inst": device(place, depth)})
        return carry

    lax.fori_loop(0, PLANE, greet, 0)
    lax.fori_loop(1, PLANE, greet_plane, 0)
    for k in range(3):
        other = lax.rem(column + 1 + k, 4)
        pl.semaphore_signal(barrier, inc=1, device_id={"tp": other * 2 + side})
    pl.semaphore_signal(barrier, inc=1, device_id={"tp": column * 2 + 1 - side})

    small = [
        pltpu.make_async_copy(src, dst, small_sem.at[n])
        for n, (src, dst) in enumerate(
            [
                (queries_hbm, queries),
                (newest_hbm, newest),
                (plan_hbm, plan),
                (counts_hbm, counts),
                (lengths_hbm, lengths),
                (moving_hbm, moving),
                (copied_hbm, copied),
            ]
        )
    ]
    for copy in small:
        copy.start()
    cache_loads = []
    for g in range(GROUPS):
        part = pl.ds(g * GROUP * TILES, GROUP * TILES)
        cache_loads.append(
            pltpu.make_async_copy(cache_hbm.at[part], cache.at[part], cache_sem.at[g])
        )
        cache_loads[-1].start()
    weight_loads = []
    for k in range(4):
        target = lax.rem(column + 1 + k, 4)
        weight_loads.append(
            pltpu.make_async_copy(
                weight_hbm.at[:, pl.ds(pl.multiple_of(target * WIDE, WIDE), WIDE)],
                weight.at[k],
                weight_sem.at[k],
            )
        )
    landing_load = pltpu.make_async_copy(landing_hbm, landing, landing_sem.at[0])

    for copy in small:
        copy.wait()
    inst_rows = iota((INSTS, INSTS), 0)
    inst_cols = iota((INSTS, INSTS), 1)
    total = counts[0] + counts[1] + counts[2]
    for m in range(MOVING):
        hit = plan[m : m + 1, :] == inst_rows
        sender = jnp.sum(jnp.where(hit, inst_cols, 0), axis=1, keepdims=True)
        sender = jnp.minimum(sender, INSTS - 1)
        place = ((sender >> 3) << 1) + (sender & 1)
        plane = (sender >> 1) & 3
        offset = (plane - depth) & 3
        away = (plane - ((inst_rows[:, :1] >> 1) & 3)) & 3
        low, high = 2 * place, 2 * place + 1
        from_below, from_above = 2 * PLANE + place, 3 * PLANE + place
        columns = (
            jnp.where(offset == 3, from_below, low),
            jnp.where(offset == 1, from_above, high),
            jnp.where(offset == 3, from_below, high),
            jnp.where(offset == 1, from_above, low),
            jnp.sum(jnp.where(hit, total[m : m + 1, :], 0), axis=1, keepdims=True),
            jnp.where(away == 1, 3, jnp.where(away == 2, 2, 0)),
            jnp.where(away == 3, 2, jnp.where(away == 2, 3, 1)),
        )
        for n, values in enumerate(columns):
            n = n * MOVING + m
            meta_vec[0:INSTS, n : n + 1] = values
    meta_vec[INSTS : INSTS + MOVING, 0:INSTS] = total
    meta_load = pltpu.make_async_copy(meta_vec, meta, meta_sem.at[0])
    meta_load.start()

    stacked = jnp.concatenate(
        [
            queries[s, :, h * HEAD_DIM : (h + 1) * HEAD_DIM]
            for s in range(STEPS)
            for h in range(HEADS)
        ],
        axis=0,
    )
    pick = iota((ROWS, REQS * ROWS), 1) - REQS * iota((ROWS, REQS * ROWS), 0)
    order = jnp.concatenate(
        [(pick == b).astype(F32) for b in range(REQS)], axis=0
    ).astype(BF16)
    ordered[...] = jnp.dot(order, stacked, preferred_element_type=F32)
    back = iota((REQS, REQS * ROWS), 1) - ROWS * iota((REQS, REQS * ROWS), 0)
    for h in range(HEADS):
        for s in range(STEPS):
            n = (h * STEPS + s) * REQS
            regroup[n : n + REQS, :] = (back == s * HEADS + h).astype(F32).astype(BF16)
    fresh = lax.dot_general(
        ordered[...].astype(BF16),
        newest[:, :HEAD_DIM],
        (((1,), (1,)), ((), ())),
        preferred_element_type=F32,
    )
    position = iota((ROWS, TOKENS), 1)
    causal = (position >> 4) <= (iota((ROWS, TOKENS), 0) >> 3)
    for b in range(REQS):
        rows = slice(b * ROWS, (b + 1) * ROWS)
        valid = causal & ((position & (REQS - 1)) == b)
        new_scores[rows, :] = jnp.where(valid, fresh[rows] * SCALE, LOW)

    def attend_group(members):
        rows = [slice(b * ROWS, (b + 1) * ROWS) for b in members]
        stored = [
            cache[b * TILES : (b + 1) * TILES].reshape(CACHE, 2 * HEAD_DIM) for b in members
        ]
        scores = [
            lax.dot_general(
                ordered[r, :].astype(BF16),
                kv[:, :HEAD_DIM],
                (((1,), (1,)), ((), ())),
                preferred_element_type=F32,
            )
            for r, kv in zip(rows, stored)
        ]
        scores = [
            jnp.where(iota((ROWS, CACHE), 1) < lengths[b], x * SCALE, LOW)
            for b, x in zip(members, scores)
        ]
        highest = [
            jnp.maximum(
                jnp.max(x, axis=1, keepdims=True),
                jnp.max(new_scores[r, :], axis=1, keepdims=True),
            )
            for r, x in zip(rows, scores)
        ]
        weights = [jnp.exp2(x - h) for x, h in zip(scores, highest)]
        late = [jnp.exp2(new_scores[r, :] - h) for r, h in zip(rows, highest)]
        shares = [
            1.0 / (jnp.sum(w, axis=1, keepdims=True) + jnp.sum(n, axis=1, keepdims=True))
            for w, n in zip(weights, late)
        ]
        outs = [
            jnp.dot((w * x).astype(BF16), kv[:, HEAD_DIM:], preferred_element_type=F32)
            for w, x, kv in zip(weights, shares, stored)
        ]
        for r, n, x, o in zip(rows, late, shares, outs):
            new_scores[r, :] = n * x
            acc[r, :] = o

    meta_load.wait()
    tail_rows = iota((LANE_ROWS, WINDOW), 0)
    tail_cols = iota((LANE_ROWS, WINDOW), 1)
    first_tiles = []
    for m in range(MOVING):
        total = meta[INSTS + m, me]
        start = lengths[moving[0, m]] - total
        first = jnp.minimum(start // TILE, TILES - WINDOW // TILE)
        first_tiles.append(first)
        shift = (tail_cols - tail_rows == start - first * TILE) & (tail_rows < total)
        shifts[m] = shift.astype(F32).astype(BF16)

    for g in range(1):
        cache_loads[g].wait()
        if g == 0:
            for load in weight_loads:
                load.start()
            landing_load.start()
        attend_group(range(g * GROUP, (g + 1) * GROUP))
    for g in range(1, GROUPS):
        cache_loads[g].wait()

    for m in range(MOVING):
        tile = moving[0, m] * TILES + first_tiles[m]
        window = jnp.concatenate(
            [cache[tile + t] for t in range(WINDOW // TILE)], axis=0
        )
        tail = jnp.dot(shifts[m], window, preferred_element_type=F32).astype(BF16)
        for c in range(2):
            for n in range(2):
                for t in range(BATCHES):
                    first_row = n * HALF + t * TILE
                    tails[t, 2 * m + c, n] = tail[
                        first_row : first_row + TILE, c * HEAD_DIM : (c + 1) * HEAD_DIM
                    ]

    pl.semaphore_wait(barrier, 3 * PLANE - 1 + 3 + 1)

    def send(src, dst, place, plane, sems, t):
        pltpu.make_async_remote_copy(
            src_ref=src,
            dst_ref=dst,
            send_sem=sems.at[0, t],
            recv_sem=sems.at[1, t],
            device_id={"inst": device(place, plane)},
        ).start()

    def scatter(t):
        def beside(o, carry):
            place = lax.rem(spot + o, PLANE)
            send(
                tails.at[t, place, 0],
                held[t].at[2 * PLANE + spot],
                place,
                above,
                scatter_sem,
                t,
            )
            send(
                tails.at[t, place, 1],
                held[t].at[3 * PLANE + spot],
                place,
                below,
                scatter_sem,
                t,
            )
            return carry

        def within(o, carry):
            place = lax.rem(spot + o, PLANE)
            send(
                tails.at[t, place],
                held[t].at[pl.ds(2 * spot, 2)],
                place,
                depth,
                scatter_sem,
                t,
            )
            return carry

        lax.fori_loop(0, PLANE, beside, 0)
        lax.fori_loop(1, PLANE, within, 0)
        held[t][pl.ds(2 * spot, 2)] = tails[t, spot]

    for t in range(BATCHES):
        scatter(t)

    for b in range(GROUP, REQS, 6):
        attend_group(range(b, b + 6))

    context = acc[...] + jnp.dot(
        new_scores[...].astype(BF16), newest[:, HEAD_DIM:], preferred_element_type=F32
    )
    context = context.astype(BF16)
    context = jnp.dot(regroup[...], context, preferred_element_type=F32).astype(BF16)
    context = jnp.concatenate(
        [context[h * TOKENS : (h + 1) * TOKENS] for h in range(HEADS)], axis=1
    )

    wide_sends = []

    def project(k):
        weight_loads[k].wait()
        partial = jnp.dot(context, weight[k], preferred_element_type=F32)
        if k < 3:
            wide_out[k] = partial.astype(BF16)
            copy = pltpu.make_async_remote_copy(
                src_ref=wide_out.at[k],
                dst_ref=wide_in.at[k],
                send_sem=wide_send_sem.at[k],
                recv_sem=wide_recv_sem.at[k],
                device_id={"tp": lax.rem(column + 1 + k, 4) * 2 + side},
            )
            copy.start()
            wide_sends.append(copy)
        else:
            wide_own[...] = partial

    for k in range(4):
        project(k)

    def forward(t):
        wait_bytes(held[t].at[pl.ds(0, 4 * PLANE - 2)], scatter_sem.at[1, t])
        for place in range(PLANE):
            row = device(place, above)
            upward[t, place] = held[t][meta[row, 2 * MOVING + lane]]
            row = device(place, below)
            downward[t, place] = held[t][meta[row, 3 * MOVING + lane]]
            row = device(place, depth)
            inside[t, place, 0] = held[t][meta[row, lane]]
            inside[t, place, 1] = held[t][meta[row, MOVING + lane]]

        def beside(o, carry):
            place = lax.rem(spot + o, PLANE)
            send(
                upward.at[t, place],
                arrived.at[t, 4 * spot + 2],
                place,
                above,
                forward_sem,
                t,
            )
            send(
                downward.at[t, place],
                arrived.at[t, 4 * spot + 3],
                place,
                below,
                forward_sem,
                t,
            )
            return carry

        def within(o, carry):
            place = lax.rem(spot + o, PLANE)
            send(
                inside.at[t, place],
                arrived.at[t, pl.ds(4 * spot, 2)],
                place,
                depth,
                forward_sem,
                t,
            )
            return carry

        lax.fori_loop(0, PLANE, beside, 0)
        lax.fori_loop(1, PLANE, within, 0)
        arrived[t, pl.ds(4 * spot, 2)] = inside[t, spot]

    for t in range(BATCHES):
        forward(t)

    land_rows = iota((LAND_ROWS, LANE_ROWS), 0)
    land_cols = iota((LAND_ROWS, LANE_ROWS), 1)
    target_rows = iota((LAND_ROWS, 2 * HEAD_DIM), 0)
    landing_load.wait()
    for m in range(MOVING):
        first = copied[0, m]
        total_in = meta[me, 4 * MOVING + m]
        place = (land_rows - land_cols == first) & (land_cols < total_in)
        places[m] = place.astype(F32).astype(BF16)
        fits = (target_rows >= first) & (target_rows < first + total_in)
        landing[m] = jnp.where(fits, 0.0, landing[m].astype(F32)).astype(BF16)

    for k in range(3):
        pltpu.make_async_copy(wide_in.at[k], wide_in.at[k], wide_recv_sem.at[k]).wait()
    total = wide_own[...]
    for k in range(3):
        total = total + wide_in[k].astype(F32)
    left, right = total[:, :NARROW], total[:, NARROW:]
    narrow_out[...] = jnp.where(side == 0, right, left).astype(BF16)
    narrow_send = pltpu.make_async_remote_copy(
        src_ref=narrow_out,
        dst_ref=narrow_in,
        send_sem=narrow_sem.at[0],
        recv_sem=narrow_sem.at[1],
        device_id={"tp": column * 2 + 1 - side},
    )
    narrow_send.start()
    own = jnp.where(side == 0, left, right)
    narrow_send.wait_recv()
    attended[...] = (own + narrow_in[...].astype(F32)).astype(BF16)

    for t in range(BATCHES):
        wait_bytes(arrived.at[t, pl.ds(0, 4 * PLANE - 2)], forward_sem.at[1, t])

    for m in range(MOVING):
        rows = jnp.concatenate(
            [
                jnp.concatenate(
                    [
                        arrived[t, (2 * m + c) * 4 + meta[me, (5 + n) * MOVING + m]]
                        for c in range(2)
                    ],
                    axis=1,
                )
                for n in range(2)
                for t in range(BATCHES)
            ],
            axis=0,
        )
        placed = jnp.dot(places[m], rows, preferred_element_type=F32)
        landed[m] = (landing[m].astype(F32) + placed).astype(BF16)

    for copy in wide_sends:
        copy.wait_send()
    narrow_send.wait_send()
    for t in range(BATCHES):
        wait_bytes(held[t].at[pl.ds(0, 4 * PLANE - 2)], scatter_sem.at[0, t])
        wait_bytes(arrived.at[t, pl.ds(0, 4 * PLANE - 2)], forward_sem.at[0, t])


def publish(attended, landed, attended_out, landed_out, sems):
    copies = [pltpu.make_async_copy(attended, attended_out, sems.at[MOVING])] + [
        pltpu.make_async_copy(landed.at[m], landed_out.at[m], sems.at[m])
        for m in range(MOVING)
    ]
    for copy in copies:
        copy.start()
    for copy in copies:
        copy.wait()


def on_device(
    queries,
    key_values,
    new_key_values,
    cache_lengths,
    output_weight,
    moving_requests,
    migration_plan,
    row_counts,
    copied_rows,
    landing,
):
    in_hbm = pl.BlockSpec(memory_space=pltpu.HBM)
    dma = pltpu.SemaphoreType.DMA
    attended, landed = pl.pallas_call(
        main_kernel,
        out_shape=(
            jax.ShapeDtypeStruct((TOKENS, NARROW), BF16),
            jax.ShapeDtypeStruct((MOVING, LAND_ROWS, 2 * HEAD_DIM), BF16),
        ),
        in_specs=[in_hbm] * 10,
        out_specs=(
            pl.BlockSpec(memory_space=pltpu.VMEM),
            pl.BlockSpec(memory_space=pltpu.VMEM),
        ),
        scratch_shapes=[
            pltpu.SMEM((REQS,), I32),
            pltpu.SMEM((1, MOVING), I32),
            pltpu.SMEM((1, MOVING), I32),
            pltpu.VMEM((STEPS, REQS, HEADS * HEAD_DIM), BF16),
            pltpu.VMEM((TOKENS, 2 * HEAD_DIM), BF16),
            pltpu.VMEM((REQS * TILES, TILE, 2 * HEAD_DIM), BF16),
            pltpu.VMEM((4, HEADS * HEAD_DIM, WIDE), BF16),
            pltpu.VMEM((MOVING, INSTS), I32),
            pltpu.VMEM((STEPS, MOVING, INSTS), I32),
            pltpu.VMEM((MOVING, LAND_ROWS, 2 * HEAD_DIM), BF16),
            pltpu.VMEM((40, 128), I32),
            pltpu.SMEM((40, 128), I32),
            pltpu.VMEM((REQS * ROWS, HEAD_DIM), F32),
            pltpu.VMEM((REQS * ROWS, REQS * ROWS), BF16),
            pltpu.VMEM((REQS * ROWS, TOKENS), F32),
            pltpu.VMEM((REQS * ROWS, HEAD_DIM), F32),
            pltpu.VMEM((MOVING, LANE_ROWS, WINDOW), BF16),
            pltpu.VMEM((MOVING, LAND_ROWS, LANE_ROWS), BF16),
            pltpu.VMEM((BATCHES, PLANE, 2, TILE, HEAD_DIM), BF16),
            pltpu.VMEM((4 * PLANE, TILE, HEAD_DIM), BF16),
            pltpu.VMEM((4 * PLANE, TILE, HEAD_DIM), BF16),
            pltpu.VMEM((4 * PLANE, TILE, HEAD_DIM), BF16),
            pltpu.VMEM((BATCHES, PLANE, 2, TILE, HEAD_DIM), BF16),
            pltpu.VMEM((BATCHES, PLANE, TILE, HEAD_DIM), BF16),
            pltpu.VMEM((BATCHES, PLANE, TILE, HEAD_DIM), BF16),
            pltpu.VMEM((BATCHES, 4 * PLANE, TILE, HEAD_DIM), BF16),
            pltpu.VMEM((3, TOKENS, WIDE), BF16),
            pltpu.VMEM((3, TOKENS, WIDE), BF16),
            pltpu.VMEM((TOKENS, WIDE), F32),
            pltpu.VMEM((TOKENS, NARROW), BF16),
            pltpu.VMEM((TOKENS, NARROW), BF16),
            dma((7,)),
            dma((GROUPS,)),
            dma((4,)),
            dma((1,)),
            dma((1,)),
            dma((2, BATCHES)),
            dma((2, BATCHES)),
            dma((3,)),
            dma((3,)),
            dma((2,)),
        ],
        compiler_params=pltpu.CompilerParams(
            collective_id=0,
            has_side_effects=True,
            vmem_limit_bytes=40 * 1024 * 1024,
        ),
    )(
        *(
            pltpu.with_memory_space_constraint(x, pltpu.HBM)
            for x in (
                cache_lengths,
                moving_requests,
                copied_rows,
                queries,
                new_key_values.reshape(TOKENS, 2 * HEAD_DIM),
                key_values.reshape(REQS * TILES, TILE, 2 * HEAD_DIM),
                output_weight,
                migration_plan.T,
                row_counts.transpose(0, 2, 1),
                landing[0],
            )
        )
    )
    in_vmem = pl.BlockSpec(memory_space=pltpu.VMEM)
    anywhere = pl.BlockSpec(memory_space=pl.ANY)
    attended, landed = pl.pallas_call(
        publish,
        out_shape=(
            jax.ShapeDtypeStruct(attended.shape, BF16),
            jax.ShapeDtypeStruct(landed.shape, BF16),
        ),
        in_specs=[in_vmem, in_vmem],
        out_specs=(anywhere, anywhere),
        scratch_shapes=[dma((MOVING + 1,))],
        compiler_params=pltpu.CompilerParams(vmem_limit_bytes=4 * 1024 * 1024),
    )(
        pltpu.with_memory_space_constraint(attended, pltpu.VMEM),
        pltpu.with_memory_space_constraint(landed, pltpu.VMEM),
    )
    return attended.reshape(STEPS, REQS, NARROW), landed[None]


def solution(mesh):
    placed = (
        P(None, "inst", "tp"),
        P("inst", None, "tp"),
        P(None, "inst", "tp"),
        P("inst"),
        P("tp", None),
        P("inst", None),
        P(),
        P(),
        P("inst", None),
        P("inst", None, None, "tp"),
    )
    return jax.shard_map(
        on_device,
        mesh=mesh,
        in_specs=placed,
        out_specs=(P(None, "inst", "tp"), P("inst", None, None, "tp")),
        check_vma=False,
    )
```
